256 devices in a mesh: section: 4 (over z_lo, core), dp: 4 (over y), vocab: 16 (over z_hi, x).
Axes of the slice: x: 4, y: 4, z: 8 (z_hi: 4, z_lo: 2; z = z_hi * 2 + z_lo), core: 2. Of those that a mesh axis runs over, the one named last changes fastest.
Arguments:
- hidden: bfloat16 [1024, 5120], P('dp', ('section', 'vocab')), may hold values from -1.5 to 1.5
- norm_gain: bfloat16 [5120], P(('section', 'vocab')), may hold values from 0.5 to 1.5
- head: bfloat16 [5120, 151936], P('dp', ('section', 'vocab')), may hold values from -0.25 to 0.25
- token_ids: int32 [1024], P('dp'), may hold values from 0 to 151935
- entropy_mask: int32 [1024], P('dp'), may hold values 0 or 1
- group_ids: int32 [1024], P('dp'), may hold values from 0 to 31, as said below
- old_logp: float32 [1024], P('dp'), may hold values from -30 to 0
- scores: float32 [1024], P('dp'), may hold values from -6 to 6
Outputs:
- new_logp: float32 [1024], P('dp')
- entropy: float32 [1024], P('dp')
- grad_hidden: bfloat16 [1024, 5120], P('dp', ('section', 'vocab'))
The draws below stay inside these ranges and needn't reach their ends.
Inputs may be any that keep to these rules, and one draw needn't show every extreme that they name: `group_ids`: tokens of the i-th block of 256 rows carry group ids from i * 8 to (i + 1) * 8 - 1, each of these at least once.
All inputs are finite; a program needn't handle non-finite values. No bound on the sum of `entropy_mask` on one device may be relied on, other than what follows from the above.
Results may differ from the reference program's by a relative error of at most 0.0095.
Values may be sent and summed in bfloat16 or wider, within the bound.
No kernel may reach another device: no remote copies, remote signals or barrier semaphores. Data moves between devices by JAX's collectives and lax.ppermute only.
A program may use at most 128 MiB of HBM per device.

```python
import math
import jax
import jax.numpy as jnp
from jax import lax

D = 5120
V = 151936
TR = 256
GPD = 8
TOKENS = 1024


def shared_parts(key):
    base = jax.random.fold_in(key, 7)
    direction = jnp.clip(jax.random.normal(jax.random.fold_in(base, 1), (D,), jnp.float32), -2.0, 2.0)
    first_col = jax.random.randint(jax.random.fold_in(base, 2), (), 0, V)
    second_col = (first_col + V // 2 + jax.random.randint(jax.random.fold_in(base, 3), (), 0, V // 4)) % V
    return (direction, first_col, second_col)


def draw_head(key, part):
    direction, first_col, second_col = shared_parts(key)
    key = jax.random.fold_in(key, 11)
    spread = 3.0 / math.sqrt(D)
    values = jax.random.normal(jax.random.fold_in(key, 1), (D, V), jnp.float32) * spread
    values = jnp.clip(values, -0.2, 0.2)
    columns = jnp.arange(V, dtype=jnp.int32)[None, :]
    strong = 250.0 / D
    values = jnp.where(columns == first_col, strong * direction[:, None], values)
    values = jnp.where(columns == second_col, 0.99 * strong * direction[:, None], values)
    bound = max(0.2, 500.0 / D)
    return jnp.clip(values, -bound, bound).astype(jnp.bfloat16)


def draw_hidden(key, part):
    direction, first_col, second_col = shared_parts(key)
    key = jax.random.fold_in(key, 13)
    noise = jax.random.normal(jax.random.fold_in(key, 1), (TOKENS, D), jnp.float32)
    drawn = 0.1 * noise
    chosen = jax.random.randint(jax.random.fold_in(key, 4), (TOKENS, 1), 0, 8) == 0
    strength = jax.random.uniform(jax.random.fold_in(key, 5), (TOKENS, 1), jnp.float32, 0.5, 5.0)
    aligned = 0.1 * (strength * direction[None, :] + noise)
    values = jnp.where(chosen, aligned, drawn)
    return jnp.clip(values, -1.5, 1.5).astype(jnp.bfloat16)


def draw_group_ids(key, part):
    key = jax.random.fold_in(key, 17)
    block_total = TOKENS // TR

    def block_ids(block_key, block_index):
        order = jax.random.permutation(jax.random.fold_in(block_key, 1), TR)
        extra = jax.random.randint(jax.random.fold_in(block_key, 2), (TR,), 0, GPD)
        local_ids = jnp.where(order < GPD, order, extra)
        return local_ids + block_index * GPD
    block_keys = jax.random.split(key, block_total)
    result = jax.vmap(block_ids)(block_keys, jnp.arange(block_total, dtype=jnp.int32))
    return result.reshape(TOKENS).astype(jnp.int32)


def draw_old_logp(key, part):
    key = jax.random.fold_in(key, 19)
    center = -math.log(V) - 4.5
    offset = jnp.clip(1.5 * jax.random.normal(jax.random.fold_in(key, 1), (TOKENS,), jnp.float32), -3.0, 3.0)
    return (center + offset).astype(jnp.float32)


def place_ends(entries, own_key, smallest, largest):
    longest = entries.shape.index(max(entries.shape))
    spots = []
    for shift in (0, 1):
        where = [jax.random.randint(jax.random.fold_in(own_key, axis), (), 0, length) for axis, length in enumerate(entries.shape)]
        where[longest] = (where[longest] + shift) % entries.shape[longest]
        spots.append(tuple(where))
    return entries.at[spots[0]].set(smallest).at[spots[1]].set(largest)


def steps_of(own_key, extent, pieces, smallest, high):
    factor_of = 1.0
    for position, shards_of in pieces:
        heights = jax.random.uniform(jax.random.fold_in(jax.random.fold_in(own_key, 6), position), (shards_of,), jnp.float32, smallest / len(pieces), high / len(pieces))
        factor_of = factor_of * jnp.repeat(jnp.exp(heights), extent[position] // shards_of).reshape((-1,) + (1,) * (len(extent) - 1 - position))
    return factor_of


def bell_draw(key, dims, scale, limit, pieces=(), kind=jnp.bfloat16):
    level = steps_of(key, dims, pieces, -0.22, 0.18) if pieces else 1.0
    values = jax.random.normal(key, dims, jnp.float32) * scale * level
    return jnp.minimum(jnp.maximum(values, -limit), limit).astype(kind)


def setup_inputs(seed: int = 0) -> dict:
    key_of = jax.random.split(jax.random.key(seed), 9)
    return {
        "hidden": draw_hidden(jax.random.fold_in(key_of[8], 71), 0),
        "norm_gain": jnp.clip(1.0 + 0.1 * jax.random.normal(key_of[1], (D,), jnp.float32), 0.5, 1.5).astype(jnp.bfloat16),
        "head": draw_head(jax.random.fold_in(key_of[8], 71), 0),
        "token_ids": place_ends(jax.random.randint(key_of[3], (TOKENS,), 0, V), jax.random.fold_in(key_of[3], 1), 0, V - 1).astype(jnp.int32),
        "entropy_mask": place_ends((jax.random.randint(key_of[4], (TOKENS,), 0, 5) < 1).astype(jnp.int32), jax.random.fold_in(key_of[4], 1), 0, 1),
        "group_ids": draw_group_ids(jax.random.fold_in(key_of[8], 71), 0),
        "old_logp": draw_old_logp(jax.random.fold_in(key_of[8], 71), 0),
        "scores": bell_draw(key_of[7], (TOKENS,), 1.0, 6.0, ((0, 4),), jnp.float32),
    }


NORM_EPSILON = 1e-06
LOW_CLIP = 0.5
HIGH_CLIP = 2.0

def reference(hidden, norm_gain, head, token_ids, entropy_mask, group_ids, old_logp, scores):
    group_total = GPD * (TOKENS // TR)
    unit_counts = jnp.ones_like(scores)
    group_sum = jax.ops.segment_sum(scores, group_ids, num_segments=group_total)
    group_count = jax.ops.segment_sum(unit_counts, group_ids, num_segments=group_total)
    advantage = scores - (group_sum / group_count)[group_ids]
    hidden_float = hidden.astype(jnp.float32)
    inverse = lax.rsqrt(lax.optimization_barrier(jnp.mean(hidden_float * hidden_float, axis=1, keepdims=True)) + NORM_EPSILON)
    unit_rows = hidden_float * inverse
    gain_float = norm_gain.astype(jnp.float32)
    normed = (unit_rows * gain_float).astype(jnp.bfloat16)

    def one_block(block_index):
        row_start = block_index * TR
        block_rows = lax.dynamic_slice_in_dim(normed, row_start, TR, 0)
        block_ids = lax.dynamic_slice_in_dim(token_ids, row_start, TR, 0)
        block_mask = lax.dynamic_slice_in_dim(entropy_mask, row_start, TR, 0)
        block_old = lax.dynamic_slice_in_dim(old_logp, row_start, TR, 0)
        block_adv = lax.dynamic_slice_in_dim(advantage, row_start, TR, 0)
        logits = jnp.dot(block_rows, head, preferred_element_type=jnp.float32)
        row_top = lax.optimization_barrier(jnp.max(logits, axis=1))
        shifted = jnp.exp(logits - row_top[:, None])
        exp_total = lax.optimization_barrier(jnp.sum(shifted, axis=1))
        weighted = lax.optimization_barrier(jnp.sum(shifted * logits, axis=1))
        is_target = jnp.arange(V, dtype=jnp.int32)[None, :] == block_ids[:, None]
        target = lax.optimization_barrier(jnp.sum(jnp.where(is_target, logits, 0.0), axis=1))
        log_total = row_top + jnp.log(exp_total)
        block_entropy = log_total - weighted / exp_total
        block_logp = target - log_total
        weight = jnp.clip(jnp.exp(block_logp - block_old), LOW_CLIP, HIGH_CLIP)
        grad_logp = -block_mask.astype(jnp.float32) * weight * block_adv
        softmax_probs = shifted / exp_total[:, None]
        grad_logits = (grad_logp[:, None] * (is_target.astype(jnp.float32) - softmax_probs)).astype(jnp.bfloat16)
        grad_normed = jnp.dot(grad_logits, head.T, preferred_element_type=jnp.float32)
        return (block_logp, block_entropy, grad_normed)
    block_logp, block_entropy, grad_normed = lax.map(one_block, jnp.arange(TOKENS // TR, dtype=jnp.int32))
    grad_normed = grad_normed.reshape(TOKENS, D)
    inner_mean = lax.optimization_barrier(jnp.mean(unit_rows * gain_float * grad_normed, axis=1, keepdims=True))
    grad_hidden = (inverse * (gain_float * grad_normed - unit_rows * inner_mean)).astype(jnp.bfloat16)
    return (block_logp.reshape(TOKENS), block_entropy.reshape(TOKENS), grad_hidden)
```

```python
import functools

import jax
import jax.numpy as jnp
from jax import lax
from jax.experimental import pallas as pl
from jax.experimental.pallas import tpu as pltpu
from jax.sharding import PartitionSpec as P

NORM_EPSILON = 1e-06
LOW_CLIP = 0.5
HIGH_CLIP = 2.0
GPD = 8
CHUNK = 80
TILE = 400
EXTRA = 16
HALF_TILES = 3
BIG = 32000.0
REL = (1, 3, 2, 0)
SECTION, DP, VOCAB = "section", "dp", "vocab"
f32, bf16, i16, i32 = jnp.float32, jnp.bfloat16, jnp.int16, jnp.int32
CORE_SWAP = ((0, 1), (1, 0), (2, 3), (3, 2))
LOW_SWAP = ((0, 2), (1, 3), (2, 0), (3, 1))
UP = tuple((i, (i + 1) % 4) for i in range(4))
DOWN = tuple((i, (i + 3) % 4) for i in range(4))
ACROSS = tuple((i, (i + 2) % 4) for i in range(4))
X_GROUPS = [[z * 4 + x for x in range(4)] for z in range(4)]
Z_GROUPS = [[z * 4 + x for z in range(4)] for x in range(4)]
CORE_GROUPS = [[(z * 2 + c) * 16 + v for z in range(2) for v in range(16)] for c in range(2)]
SPREAD = tuple((d * 4 + (d + REL[s]) % 4, s * 4 + d) for s in range(4) for d in range(4))
COLLECT = tuple((b, a) for a, b in SPREAD)
PARAMS = pltpu.CompilerParams(vmem_limit_bytes=32 * 1024 * 1024)


def decode(block):
    codes = block[:TILE].astype(f32)
    power = block[TILE : TILE + EXTRA].astype(f32)[:1]
    return codes * (jnp.exp2(power - 15.0) * (32768.0 / BIG))


def message_kernel(rows, half_ref, head_ref, x_ref, *rest):
    out_ref = rest[-1]
    part = jnp.dot(head_ref[...], x_ref[...], preferred_element_type=f32)
    if len(rest) == 2:
        part = part + decode(rest[0][...])
    start = (half_ref[0] * HALF_TILES + pl.program_id(0)) * TILE
    index = lax.broadcasted_iota(i32, part.shape, 0) + start
    part = jnp.where(index < rows, part, 0.0)
    top = jnp.max(jnp.abs(part), axis=0, keepdims=True)
    power = jnp.clip(jnp.floor(jnp.log2(jnp.maximum(top, 1e-30))) + 1.0, -90.0, 90.0)
    codes = part * (jnp.exp2(15.0 - power) * (BIG / 32768.0))
    codes = jnp.clip(jnp.round(codes), -32767.0, 32767.0)
    out_ref[:TILE] = codes.astype(i32).astype(i16)
    out_ref[TILE:] = jnp.broadcast_to(power, (EXTRA, part.shape[1])).astype(i32).astype(i16)


def message(head_t, x, half, arrived=None):
    rows, feats = head_t.shape
    tokens = x.shape[1]
    block = TILE + EXTRA
    in_specs = [
        pl.BlockSpec((TILE, feats), lambda i, h: (h[0] * HALF_TILES + i, 0)),
        pl.BlockSpec((feats, tokens), lambda i, h: (0, 0)),
    ]
    operands = [head_t, x]
    if arrived is not None:
        in_specs.append(pl.BlockSpec((block, tokens), lambda i, h: (i, 0)))
        operands.append(arrived)
    return pl.pallas_call(
        functools.partial(message_kernel, rows),
        out_shape=jax.ShapeDtypeStruct((HALF_TILES * block, tokens), i16),
        grid_spec=pltpu.PrefetchScalarGridSpec(
            num_scalar_prefetch=1,
            grid=(HALF_TILES,),
            in_specs=in_specs,
            out_specs=pl.BlockSpec((block, tokens), lambda i, h: (i, 0)),
        ),
        compiler_params=PARAMS,
        cost_estimate=pl.CostEstimate(
            flops=rows * feats * tokens, bytes_accessed=rows * feats, transcendentals=0
        ),
    )(half.reshape(1), *operands)


def finish_kernel(rows, head_ref, x_ref, a1, a2, b1, b2, inv_ref, target_ref, e_ref, stats_ref, logits):
    step = pl.program_id(0)
    part = jnp.dot(head_ref[...], x_ref[...], preferred_element_type=f32)
    first = step < HALF_TILES
    part = part + decode(jnp.where(first, a1[...], b1[...]))
    part = part + decode(jnp.where(first, a2[...], b2[...]))
    value = part * inv_ref[...]
    index = lax.broadcasted_iota(i32, part.shape, 0) + step * TILE
    logits[pl.ds(pl.multiple_of(step * TILE, TILE), TILE), :] = jnp.where(index < rows, value, -1e30)

    @pl.when(step == 2 * HALF_TILES - 1)
    def _():
        tokens = part.shape[1]
        top = jnp.max(logits[...], axis=0, keepdims=True)
        total = jnp.zeros((1, tokens), f32)
        weighted = jnp.zeros((1, tokens), f32)
        target = jnp.zeros((1, tokens), f32)
        for tile in range(2 * HALF_TILES):
            at = tile * TILE
            size = min(TILE, rows - at)
            block = logits[at : at + TILE, :]
            e = jnp.exp(block - top)
            place = lax.broadcasted_iota(i32, block.shape, 0) + at
            total += jnp.sum(e, axis=0, keepdims=True)
            weighted += jnp.sum(e * block, axis=0, keepdims=True)
            target += jnp.sum(jnp.where(place == target_ref[...], block, 0.0), axis=0, keepdims=True)
            e_ref[at : at + size, :] = e[:size].astype(bf16)
        stats_ref[...] = jnp.concatenate([top, total, weighted, target], axis=0)


def finish(head_t, x, a1, a2, b1, b2, inverse, target):
    rows, feats = head_t.shape
    tokens = x.shape[1]
    block = TILE + EXTRA
    low = lambda i: (jnp.minimum(i, HALF_TILES - 1), 0)
    high = lambda i: (jnp.maximum(i - HALF_TILES, 0), 0)
    whole = lambda i: (0, 0)
    return pl.pallas_call(
        functools.partial(finish_kernel, rows),
        out_shape=(jax.ShapeDtypeStruct((rows, tokens), bf16), jax.ShapeDtypeStruct((4, tokens), f32)),
        grid=(2 * HALF_TILES,),
        in_specs=[
            pl.BlockSpec((TILE, feats), lambda i: (i, 0)),
            pl.BlockSpec((feats, tokens), whole),
            pl.BlockSpec((block, tokens), low),
            pl.BlockSpec((block, tokens), low),
            pl.BlockSpec((block, tokens), high),
            pl.BlockSpec((block, tokens), high),
            pl.BlockSpec((1, tokens), whole),
            pl.BlockSpec((1, tokens), whole),
        ],
        out_specs=(pl.BlockSpec((rows, tokens), whole), pl.BlockSpec((4, tokens), whole)),
        scratch_shapes=[pltpu.VMEM((2 * HALF_TILES * TILE, tokens), f32)],
        compiler_params=PARAMS,
        cost_estimate=pl.CostEstimate(
            flops=2 * rows * feats * tokens, bytes_accessed=2 * rows * feats, transcendentals=rows * tokens
        ),
    )(head_t, x, a1, a2, b1, b2, inverse, target)


def share(value, axes, count, groups=None):
    copies = jnp.broadcast_to(value[None], (count, *value.shape))
    return lax.all_to_all(copies, axes, 0, 0, tiled=True, axis_index_groups=groups)


def shards(hidden, norm_gain, head, token_ids, entropy_mask, group_ids, old_logp, scores):
    tokens, share_cols = hidden.shape
    feats, vocab_cols = head.shape
    section, dp = lax.axis_index(SECTION), lax.axis_index(DP)
    core, low = section % 2, section // 2
    slice_index = lax.axis_index((SECTION, VOCAB))
    head_t = head.T
    hidden_t = hidden.T.astype(f32)
    gain = norm_gain.astype(f32)[:, None]

    own = (hidden_t * gain).astype(bf16)
    own = lax.ppermute(own, (SECTION, DP), SPREAD)
    own = share(own, VOCAB, 4, Z_GROUPS)
    own = share(own, VOCAB, 4, X_GROUPS)
    own = own.swapaxes(0, 1).reshape(feats, tokens)
    far = lax.ppermute(own, SECTION, LOW_SWAP)
    pair = lax.ppermute(own, SECTION, CORE_SWAP)
    far_pair = lax.ppermute(far, SECTION, CORE_SWAP)
    is_low, is_even = low == 0, core == 0
    first, second = jnp.where(is_even, own, pair), jnp.where(is_even, pair, own)
    first_far, second_far = jnp.where(is_even, far, far_pair), jnp.where(is_even, far_pair, far)

    up1 = lax.ppermute(message(head_t, first, low), DP, UP)
    down_msg1 = message(head_t, jnp.where(is_low, second, first), 1 - low)
    down1 = lax.ppermute(down_msg1, DP, DOWN)

    squares = jnp.sum(hidden_t * hidden_t, axis=0)[None]
    squares, _ = lax.optimization_barrier((squares, down_msg1[:16, :128]))
    mean_square = jnp.sum(share(squares, (SECTION, VOCAB), 64), axis=0) / (share_cols * 64)
    inverse = lax.rsqrt(mean_square + NORM_EPSILON)

    up2 = lax.ppermute(message(head_t, first_far, 1 - low), DP, UP)
    down2 = lax.ppermute(message(head_t, jnp.where(is_low, first_far, second_far), low), DP, DOWN)
    up_first, down_first = jnp.where(is_low, up2, up1), jnp.where(is_low, down2, down1)
    up_direct, down_direct = jnp.where(is_low, up1, up2), jnp.where(is_low, down1, down2)
    one, zero = jnp.ones((), i32), jnp.zeros((), i32)
    rows_up = jnp.where(is_low, first, first_far)
    rows_down = jnp.where(is_low, second, second_far)
    up3 = lax.ppermute(message(head_t, rows_up, one, up_first), DP, UP)
    down3 = lax.ppermute(message(head_t, rows_down, zero, down_first), DP, DOWN)
    rows_own = jnp.where(is_low, second_far, second)
    local_target = token_ids - slice_index * vocab_cols
    local_target = jnp.where(local_target < vocab_cols, local_target, -1)
    exps, stats = finish(
        head_t, rows_own, up_direct, down3, down_direct, up3, inverse, local_target[None]
    )

    chosen = entropy_mask != 0
    position = jnp.where(chosen, jnp.cumsum(chosen.astype(i32)) - 1, -1)
    count = jnp.sum(chosen.astype(i32))
    slots = jnp.arange(CHUNK, dtype=i32)

    def gather_rows(chunk):
        pick = position[None, :] == (slots + chunk * CHUNK)[:, None]
        mine = lax.dot_general(
            pick.astype(bf16), exps, (((1,), (1,)), ((), ())), preferred_element_type=f32
        ).astype(bf16)
        from_below = lax.ppermute(mine, DP, UP)
        from_above = lax.ppermute(mine, DP, DOWN)
        from_across = lax.ppermute(mine, DP, ACROSS)
        return pick, jnp.stack([from_above, from_below, from_across, mine])

    pick0, rows0 = gather_rows(0)

    every = share(stats, (SECTION, VOCAB), 64)
    row_top = jnp.max(every[:, 0], axis=0)
    scale = jnp.exp(every[:, 0] - row_top)
    exp_total = jnp.sum(scale * every[:, 1], axis=0)
    weighted = jnp.sum(scale * every[:, 2], axis=0)
    target = jnp.sum(every[:, 3], axis=0)
    log_total = row_top + jnp.log(exp_total)
    mean_logit = weighted / exp_total
    entropy = log_total - mean_logit
    new_logp = target - log_total
    first_group = dp * GPD
    members = (
        group_ids[:, None] == first_group + jnp.arange(GPD, dtype=i32)[None, :]
    ).astype(f32)
    group_sum = jnp.sum(scores[:, None] * members, axis=0)
    group_count = jnp.sum(members, axis=0)
    advantage = scores - jnp.sum(members * (group_sum / group_count)[None], axis=1)
    weight = jnp.clip(jnp.exp(new_logp - old_logp), LOW_CLIP, HIGH_CLIP)
    grad_logp = -entropy_mask.astype(f32) * weight * advantage
    soft = -grad_logp * jnp.exp(stats[0] - row_top) / exp_total

    def chunk_grad(pick, rows):
        values = jnp.stack([soft, grad_logp, token_ids.astype(f32), jnp.broadcast_to(count.astype(f32), soft.shape)])
        picked = jnp.sum(jnp.where(pick[None], values[:, None, :], 0.0), axis=2)
        picked = picked.at[3].set(count.astype(f32))
        factors = share(picked, DP, 4)
        most = jnp.max(factors[:, 3, 0]).astype(i32)
        factors = jnp.stack([lax.dynamic_index_in_dim(factors, (dp + r) % 4, 0, False) for r in REL])
        columns = slice_index * vocab_cols + jnp.arange(vocab_cols, dtype=i32)
        is_target = columns[None, None, :] == factors[:, 2].astype(i32)[:, :, None]
        grad_logits = factors[:, 0, :, None] * rows.astype(f32) + jnp.where(
            is_target, factors[:, 1, :, None], 0.0
        )
        grad = jnp.dot(
            grad_logits.astype(bf16).reshape(4 * CHUNK, vocab_cols), head_t, preferred_element_type=f32
        ).astype(bf16)
        grad = grad.reshape(4, CHUNK, 16, share_cols).transpose(0, 2, 3, 1)
        keep = lax.dynamic_slice_in_dim(grad.reshape(2, 2, 16, share_cols, CHUNK), core, 1, 1)[:, 0]
        give = lax.dynamic_slice_in_dim(grad.reshape(2, 2, 16, share_cols, CHUNK), 1 - core, 1, 1)[:, 0]
        grad = (keep.astype(f32) + lax.ppermute(give, SECTION, CORE_SWAP).astype(f32)).astype(bf16)
        grad = grad.reshape(32, share_cols, CHUNK)
        grad = lax.all_to_all(
            grad, (SECTION, VOCAB), 0, 0, tiled=True, axis_index_groups=CORE_GROUPS
        )
        grad = jnp.sum(grad.astype(f32), axis=0)
        grad = lax.ppermute(grad, (SECTION, DP), COLLECT)
        grad = jnp.dot(grad, pick.astype(f32), precision=lax.Precision.HIGHEST)
        return grad, most

    grad, most = chunk_grad(pick0, rows0)

    def more(state):
        chunk, total = state
        part, _ = chunk_grad(*gather_rows(chunk))
        return chunk + 1, total + part

    _, grad = lax.while_loop(lambda state: state[0] * CHUNK < most, more, (jnp.ones((), i32), grad))

    inner = grad_logp * (target - mean_logit) / (share_cols * 64)
    unit = hidden_t * inverse
    grad_hidden = inverse * (gain * grad - unit * inner[None])
    return new_logp, entropy, grad_hidden.astype(bf16).T


def solution(mesh):
    in_specs = (
        P("dp", ("section", "vocab")),
        P(("section", "vocab")),
        P("dp", ("section", "vocab")),
        P("dp"),
        P("dp"),
        P("dp"),
        P("dp"),
        P("dp"),
    )
    out_specs = (P("dp"), P("dp"), P("dp", ("section", "vocab")))
    return jax.shard_map(shards, mesh=mesh, in_specs=in_specs, out_specs=out_specs, check_vma=False)
```

```python
import functools

import jax
import jax.numpy as jnp
from jax import lax
from jax.experimental import pallas as pl
from jax.experimental.pallas import tpu as pltpu
from jax.sharding import PartitionSpec as P

NORM_EPSILON = 1e-06
LOW_CLIP = 0.5
HIGH_CLIP = 2.0
GPD = 8
CHUNK = 80
SPLIT = 48
TILE = 400
EXTRA = 16
HALF_TILES = 3
BIG = 32000.0
REL = (3, 1, 2, 0)
SECTION, DP, VOCAB = "section", "dp", "vocab"
f32, bf16, i16, i32 = jnp.float32, jnp.bfloat16, jnp.int16, jnp.int32
CORE_SWAP = ((0, 1), (1, 0), (2, 3), (3, 2))
UP = tuple((i, (i + 1) % 4) for i in range(4))
DOWN = tuple((i, (i + 3) % 4) for i in range(4))
X_GROUPS = [[z * 4 + x for x in range(4)] for z in range(4)]
Z_GROUPS = [[(a * 2 + c) * 16 + b * 4 + x for a in range(2) for b in range(4)] for c in range(2) for x in range(4)]
STEP = tuple((s * 4 + d, s * 4 + (d + (3 if s % 2 else 1)) % 4) for s in range(4) for d in range(4))
CORE_GROUPS = [[(z * 2 + c) * 16 + v for z in range(2) for v in range(16)] for c in range(2)]
SPREAD = tuple((d * 4 + (d + REL[s]) % 4, s * 4 + d) for s in range(4) for d in range(4))
COLLECT = tuple((b, a) for a, b in SPREAD)
SMALL = pltpu.CompilerParams(vmem_limit_bytes=10 * 1024 * 1024)
LARGE = pltpu.CompilerParams(vmem_limit_bytes=20 * 1024 * 1024)


def decode(block):
    codes = block[:TILE].astype(f32)
    power = block[TILE : TILE + EXTRA].astype(f32)[:1]
    return codes * (jnp.exp2(power - 15.0) * (32768.0 / BIG))


def encode(part, square_sum, out_ref):
    top = jnp.max(jnp.abs(part), axis=0, keepdims=True)
    power = jnp.clip(jnp.floor(jnp.log2(jnp.maximum(top, 1e-30))) + 1.0, -90.0, 90.0)
    codes = part * (jnp.exp2(15.0 - power) * (BIG / 32768.0))
    codes = jnp.clip(jnp.round(codes), -32767.0, 32767.0)
    sum_power = jnp.clip(jnp.floor(jnp.log2(jnp.maximum(square_sum, 1e-30))) + 1.0, -100.0, 100.0)
    scaled = square_sum * jnp.exp2(15.0 - sum_power)
    high = jnp.minimum(jnp.floor(scaled), 32767.0)
    spare = jnp.zeros((EXTRA - 4, part.shape[1]), f32)
    extra = jnp.concatenate([power, sum_power, high, jnp.round((scaled - high) * 16384.0), spare], axis=0)
    out_ref[:TILE] = codes.astype(i32).astype(i16)
    out_ref[TILE:] = extra.astype(i32).astype(i16)


def decode_sum(block):
    extra = block[TILE : TILE + EXTRA].astype(f32)
    return (extra[2:3] + extra[3:4] * (1.0 / 16384.0)) * jnp.exp2(extra[1:2] - 15.0)


def inside(part, rows, start):
    index = lax.broadcasted_iota(i32, part.shape, 0) + start
    return jnp.where(index < rows, part, 0.0)


def first_kernel(rows, half, head_ref, x_ref, sum_ref, out_ref):
    part = jnp.dot(head_ref[...], x_ref[...], preferred_element_type=f32)
    encode(inside(part, rows, (half * HALF_TILES + pl.program_id(0)) * TILE), sum_ref[...], out_ref)


def first_message(head_t, x, square_sum, half):
    rows, feats = head_t.shape
    tokens = x.shape[1]
    block = TILE + EXTRA
    return pl.pallas_call(
        functools.partial(first_kernel, rows, half),
        out_shape=jax.ShapeDtypeStruct((HALF_TILES * block, tokens), i16),
        grid=(HALF_TILES,),
        in_specs=[
            pl.BlockSpec((TILE, feats), lambda i: (half * HALF_TILES + i, 0)),
            pl.BlockSpec((feats, tokens), lambda i: (0, 0)),
            pl.BlockSpec((1, tokens), lambda i: (0, 0)),
        ],
        out_specs=pl.BlockSpec((block, tokens), lambda i: (i, 0)),
        compiler_params=SMALL,
        cost_estimate=pl.CostEstimate(
            flops=rows * feats * tokens, bytes_accessed=4 * rows * feats, transcendentals=0
        ),
    )(head_t, x, square_sum)


def message_kernel(part_ref, sum_ref, arrived_ref, out_ref):
    arrived = arrived_ref[...]
    encode(part_ref[...] + decode(arrived), sum_ref[...] + decode_sum(arrived), out_ref)


def message(part, square_sum, half, arrived):
    tokens = part.shape[1]
    block = TILE + EXTRA
    return pl.pallas_call(
        message_kernel,
        out_shape=jax.ShapeDtypeStruct(arrived.shape, i16),
        grid=(HALF_TILES,),
        in_specs=[
            pl.BlockSpec((TILE, tokens), lambda i: (half * HALF_TILES + i, 0)),
            pl.BlockSpec((1, tokens), lambda i: (0, 0)),
            pl.BlockSpec((block, tokens), lambda i: (i, 0)),
        ],
        out_specs=pl.BlockSpec((block, tokens), lambda i: (i, 0)),
        compiler_params=SMALL,
        cost_estimate=pl.CostEstimate(
            flops=8 * arrived.size, bytes_accessed=8 * arrived.size, transcendentals=0
        ),
    )(part, square_sum, arrived)


def base_kernel(rows, head_ref, x_ref, out_ref):
    part = jnp.dot(head_ref[...], x_ref[...], preferred_element_type=f32)
    out_ref[...] = inside(part, rows, pl.program_id(0) * TILE)


def base(head_t, x):
    rows, feats = head_t.shape
    tokens = x.shape[1]
    return pl.pallas_call(
        functools.partial(base_kernel, rows),
        out_shape=jax.ShapeDtypeStruct((2 * HALF_TILES * TILE, tokens), f32),
        grid=(2 * HALF_TILES,),
        in_specs=[
            pl.BlockSpec((TILE, feats), lambda i: (i, 0)),
            pl.BlockSpec((feats, tokens), lambda i: (0, 0)),
        ],
        out_specs=pl.BlockSpec((TILE, tokens), lambda i: (i, 0)),
        compiler_params=SMALL,
        cost_estimate=pl.CostEstimate(
            flops=2 * rows * feats * tokens, bytes_accessed=2 * rows * feats, transcendentals=0
        ),
    )(head_t, x)


def finish_kernel(rows, feats, base_ref, a_ref, b_ref, sum_ref, target_ref, pick_ref, e_ref, mine_ref, stats_ref, logits, exps):
    tokens = base_ref.shape[1]
    block = TILE + EXTRA
    square_sum = sum_ref[...] + decode_sum(a_ref[:block, :])
    inverse = lax.rsqrt(square_sum / feats + NORM_EPSILON)
    top = jnp.full((1, tokens), -1e30, f32)
    for tile in range(2 * HALF_TILES):
        at = tile * TILE
        ref, place = (a_ref, tile) if tile < HALF_TILES else (b_ref, tile - HALF_TILES)
        value = (base_ref[at : at + TILE, :] + decode(ref[place * block : (place + 1) * block, :])) * inverse
        if at + TILE > rows:
            index = lax.broadcasted_iota(i32, value.shape, 0) + at
            value = jnp.where(index < rows, value, -1e30)
        logits[at : at + TILE, :] = value
        top = jnp.maximum(top, jnp.max(value, axis=0, keepdims=True))
    total = jnp.zeros((1, tokens), f32)
    weighted = jnp.zeros((1, tokens), f32)
    target = jnp.zeros((1, tokens), f32)
    place = lax.broadcasted_iota(i32, (TILE, tokens), 0)
    for tile in range(2 * HALF_TILES):
        at = tile * TILE
        value = logits[at : at + TILE, :]
        e = jnp.exp(value - top)
        total += jnp.sum(e, axis=0, keepdims=True)
        weighted += jnp.sum(e * value, axis=0, keepdims=True)
        target += jnp.sum(jnp.where(place == target_ref[...] - at, value, 0.0), axis=0, keepdims=True)
        exps[at : at + TILE, :] = e.astype(bf16)
    spare = exps.shape[0] - 2 * HALF_TILES * TILE
    exps[2 * HALF_TILES * TILE :, :] = jnp.zeros((spare, tokens), bf16)
    stats_ref[...] = jnp.concatenate([top, total, weighted, target, inverse], axis=0)
    mine = lax.dot_general(pick_ref[...], exps[...], (((1,), (1,)), ((), ())), preferred_element_type=f32)
    mine_ref[...] = mine[:, :rows].astype(bf16)
    e_ref[...] = exps[:rows, :]


def finish(rows, feats, total, a, b, square_sum, target, pick):
    tokens = total.shape[1]
    padded = -(-rows // 128) * 128
    return pl.pallas_call(
        functools.partial(finish_kernel, rows, float(feats)),
        out_shape=(
            jax.ShapeDtypeStruct((rows, tokens), bf16),
            jax.ShapeDtypeStruct((CHUNK, rows), bf16),
            jax.ShapeDtypeStruct((5, tokens), f32),
        ),
        scratch_shapes=[pltpu.VMEM((2 * HALF_TILES * TILE, tokens), f32), pltpu.VMEM((padded, tokens), bf16)],
        compiler_params=LARGE,
        cost_estimate=pl.CostEstimate(
            flops=2 * rows * CHUNK * tokens, bytes_accessed=10 * rows * tokens, transcendentals=rows * tokens
        ),
    )(total, a, b, square_sum, target, pick)


def grad_kernel(rows, core_ref, r0, r1, r2, r3, r4, factor_ref, head_ref, keep_ref, give_ref, left, prod):
    @pl.when(pl.program_id(0) == 0)
    def _():
        at = 0
        for ref in (r0, r1, r2, r3, r4):
            size = ref.shape[0]
            soft = factor_ref[at : at + size, 0:1]
            hard = factor_ref[at : at + size, 1:2]
            target = factor_ref[at : at + size, 2:3].astype(i32)
            index = lax.broadcasted_iota(i32, (size, rows), 1)
            value = ref[...].astype(f32) * soft + jnp.where(index == target, hard, 0.0)
            left[at : at + size, :] = value.astype(bf16)
            at += size

    out = jnp.dot(left[...], head_ref[...], preferred_element_type=f32)
    for t in range(4):
        prod[t * 128 : t * 128 + CHUNK, :] = out[t * CHUNK : (t + 1) * CHUNK]
    core = core_ref[0]
    for z in range(2):
        for ref, side in ((keep_ref, core), (give_ref, 1 - core)):
            at = pl.multiple_of((z * 2 + side) * 128, 128)
            ref[z] = prod[pl.ds(at, 128), :].T[:, :CHUNK].astype(bf16)


def grad_product(head_t, rows, factors, core):
    cols, feats = head_t.shape
    tile = 256
    out = jax.ShapeDtypeStruct((2, feats, CHUNK), bf16)
    out_spec = pl.BlockSpec((2, tile, CHUNK), lambda i, c: (0, i, 0))
    return pl.pallas_call(
        functools.partial(grad_kernel, cols),
        out_shape=(out, out),
        grid_spec=pltpu.PrefetchScalarGridSpec(
            num_scalar_prefetch=1,
            grid=(feats // tile,),
            in_specs=[
                *[pl.BlockSpec(r.shape, lambda i, c: (0, 0)) for r in rows],
                pl.BlockSpec((4 * CHUNK, factors.shape[1]), lambda i, c: (0, 0)),
                pl.BlockSpec((cols, tile), lambda i, c: (0, i)),
            ],
            out_specs=(out_spec, out_spec),
            scratch_shapes=[pltpu.VMEM((4 * CHUNK, cols), bf16), pltpu.VMEM((512, tile), f32)],
        ),
        compiler_params=LARGE,
        cost_estimate=pl.CostEstimate(
            flops=8 * CHUNK * cols * feats, bytes_accessed=4 * cols * feats, transcendentals=0
        ),
    )(core.reshape(1), *rows, factors, head_t)


def share(value, axes, count, groups=None):
    copies = jnp.broadcast_to(value[None], (count, *value.shape))
    return lax.all_to_all(copies, axes, 0, 0, tiled=True, axis_index_groups=groups)


def shards(hidden, norm_gain, head, token_ids, entropy_mask, group_ids, old_logp, scores):
    tokens, share_cols = hidden.shape
    feats, vocab_cols = head.shape
    section, dp = lax.axis_index(SECTION), lax.axis_index(DP)
    core, low = section % 2, section // 2
    slice_index = lax.axis_index((SECTION, VOCAB))
    head_t = head.T
    hidden_t = hidden.T.astype(f32)
    gain = norm_gain.astype(f32)[:, None]

    rest = jnp.sum(hidden_t * hidden_t, axis=0, keepdims=True)
    pieces = []
    for _ in range(3):
        pieces.append(lax.reduce_precision(rest, 8, 7))
        rest = rest - pieces[-1]
    own = jnp.concatenate([hidden_t * gain, *pieces, jnp.zeros((5, tokens), f32)]).astype(bf16)
    own = lax.ppermute(own, (SECTION, DP), SPREAD)
    lines = share(own, (SECTION, VOCAB), 8, Z_GROUPS)

    blocks = share(lines, VOCAB, 4, X_GROUPS).reshape(4, 2, 4, share_cols + 8, tokens)
    sums = jnp.sum(blocks[:, :, :, share_cols:].astype(f32), axis=(0, 2, 3))
    blocks = blocks[:, :, :, :share_cols].transpose(1, 2, 0, 3, 4).reshape(2, feats, tokens)

    def send(part):
        return lax.ppermute(part, (SECTION, DP), STEP)

    first, later = blocks[0], blocks[1]
    p1 = send(first_message(head_t, first, sums[:1], 0))
    q1 = send(first_message(head_t, first, sums[:1], 1))
    later_pair = lax.ppermute(later, SECTION, CORE_SWAP)
    first_pair = lax.ppermute(first, SECTION, CORE_SWAP)
    sums_pair = lax.ppermute(sums, SECTION, CORE_SWAP)
    is_even = core == 0
    second_sum, last_sum = jnp.where(is_even, sums, sums_pair)[1:], jnp.where(is_even, sums_pair, sums)[1:]
    second, last = jnp.where(is_even, later, later_pair), jnp.where(is_even, later_pair, later)
    part2, part3 = lax.optimization_barrier((base(head_t, second), base(head_t, first_pair)))
    p2 = send(message(part2, second_sum, 0, p1))
    q2 = send(message(part2, second_sum, 1, q1))
    p3 = send(message(part3, sums_pair[:1], 0, p2))
    q3 = message(part3, sums_pair[:1], 1, q2)
    q3 = send(q3)
    local_target = token_ids - slice_index * vocab_cols
    local_target = jnp.where(local_target < vocab_cols, local_target, -1)

    chosen = entropy_mask != 0
    position = jnp.where(chosen, jnp.cumsum(chosen.astype(i32)) - 1, -1)
    count = jnp.sum(chosen.astype(i32))
    slots = jnp.arange(CHUNK, dtype=i32)
    pick0 = position[None, :] == slots[:, None]

    own_part = base(head_t, last)
    exps, mine0, stats = finish(
        vocab_cols, share_cols * 64, own_part, p3, q3, last_sum, local_target[None], pick0.astype(bf16)
    )

    def send_rows(mine):
        from_below = lax.ppermute(mine, DP, UP)
        from_above = lax.ppermute(mine, DP, DOWN)
        return from_above, from_below, mine

    def gather_rows(chunk):
        pick = position[None, :] == (slots + chunk * CHUNK)[:, None]
        mine = lax.dot_general(
            pick.astype(bf16), exps, (((1,), (1,)), ((), ())), preferred_element_type=f32
        ).astype(bf16)
        return pick, send_rows(mine)

    rows0 = send_rows(mine0)

    inverse = stats[4]
    every = share(stats[:4], (SECTION, VOCAB), 64)
    row_top = jnp.max(every[:, 0], axis=0)
    scale = jnp.exp(every[:, 0] - row_top)
    exp_total = jnp.sum(scale * every[:, 1], axis=0)
    weighted = jnp.sum(scale * every[:, 2], axis=0)
    target = jnp.sum(every[:, 3], axis=0)
    log_total = row_top + jnp.log(exp_total)
    mean_logit = weighted / exp_total
    entropy = log_total - mean_logit
    new_logp = target - log_total
    first_group = dp * GPD
    members = (
        group_ids[:, None] == first_group + jnp.arange(GPD, dtype=i32)[None, :]
    ).astype(f32)
    group_sum = jnp.sum(scores[:, None] * members, axis=0)
    group_count = jnp.sum(members, axis=0)
    advantage = scores - jnp.sum(members * (group_sum / group_count)[None], axis=1)
    weight = jnp.clip(jnp.exp(new_logp - old_logp), LOW_CLIP, HIGH_CLIP)
    grad_logp = -entropy_mask.astype(f32) * weight * advantage
    soft = -grad_logp * jnp.exp(stats[0] - row_top) / exp_total

    def chunk_grad(pick, rows):
        values = jnp.stack([soft, grad_logp, token_ids.astype(f32), jnp.broadcast_to(count.astype(f32), soft.shape)])
        picked = jnp.sum(jnp.where(pick[None], values[:, None, :], 0.0), axis=2)
        picked = picked.at[3].set(count.astype(f32))
        from_above, from_below, mine = rows
        picked, from_above, from_below = lax.optimization_barrier((picked, from_above, from_below))
        across_low = lax.ppermute(from_below[:SPLIT], DP, UP)
        across_high = lax.ppermute(from_above[SPLIT:], DP, DOWN)
        rows = from_below, from_above, across_low, across_high, mine
        factors = share(picked, DP, 4)
        most = jnp.max(factors[:, 3, 0]).astype(i32)
        factors = jnp.stack([lax.dynamic_index_in_dim(factors, (dp + r) % 4, 0, False) for r in REL])
        factors = factors.transpose(0, 2, 1).reshape(4 * CHUNK, 4)
        factors = factors - jnp.array([0, 0, 1, 0], f32) * (slice_index * vocab_cols).astype(f32)
        keep, give = grad_product(head_t, rows, factors, core)
        grad = (keep.astype(f32) + lax.ppermute(give, SECTION, CORE_SWAP).astype(f32)).astype(bf16)
        grad = grad.reshape(32, share_cols, CHUNK)
        grad = lax.all_to_all(
            grad, (SECTION, VOCAB), 0, 0, tiled=True, axis_index_groups=CORE_GROUPS
        )
        grad = jnp.sum(grad.astype(f32), axis=0)
        grad = lax.ppermute(grad, (SECTION, DP), COLLECT)
        grad = jnp.dot(grad, pick.astype(f32), precision=lax.Precision.HIGHEST)
        return grad, most

    grad, most = chunk_grad(pick0, rows0)

    def more(state):
        chunk, total = state
        part, _ = chunk_grad(*gather_rows(chunk))
        return chunk + 1, total + part

    _, grad = lax.while_loop(lambda state: state[0] * CHUNK < most, more, (jnp.ones((), i32), grad))

    inner = grad_logp * (target - mean_logit) / (share_cols * 64)
    unit = hidden_t * inverse
    grad_hidden = inverse * (gain * grad - unit * inner[None])
    return new_logp, entropy, grad_hidden.astype(bf16).T


def solution(mesh):
    in_specs = (
        P("dp", ("section", "vocab")),
        P(("section", "vocab")),
        P("dp", ("section", "vocab")),
        P("dp"),
        P("dp"),
        P("dp"),
        P("dp"),
        P("dp"),
    )
    out_specs = (P("dp"), P("dp"), P("dp", ("section", "vocab")))
    return jax.shard_map(shards, mesh=mesh, in_specs=in_specs, out_specs=out_specs, check_vma=False)
```

```python
import functools

import jax
import jax.numpy as jnp
from jax import lax
from jax.experimental import pallas as pl
from jax.experimental.pallas import tpu as pltpu
from jax.sharding import PartitionSpec as P

NORM_EPSILON = 1e-06
LOW_CLIP = 0.5
HIGH_CLIP = 2.0
GPD = 8
CHUNK = 80
FEW = 64
SHARE = 80
TILE = 400
EXTRA = 16
HALF_TILES = 3
BIG = 32000.0
REL = (3, 1, 2, 0)
SECTION, DP, VOCAB = "section", "dp", "vocab"
f32, bf16, i16, i32 = jnp.float32, jnp.bfloat16, jnp.int16, jnp.int32
CORE_SWAP = ((0, 1), (1, 0), (2, 3), (3, 2))
UP = tuple((i, (i + 1) % 4) for i in range(4))
DOWN = tuple((i, (i + 3) % 4) for i in range(4))
X_GROUPS = [[z * 4 + x for x in range(4)] for z in range(4)]
Z_GROUPS = [[(a * 2 + c) * 16 + b * 4 + x for a in range(2) for b in range(4)] for c in range(2) for x in range(4)]
STEP = tuple((s * 4 + d, s * 4 + (d + (3 if s % 2 else 1)) % 4) for s in range(4) for d in range(4))
CORE_GROUPS = [[(z * 2 + c) * 16 + v for z in range(2) for v in range(16)] for c in range(2)]
SPREAD = tuple((d * 4 + (d + REL[s]) % 4, s * 4 + d) for s in range(4) for d in range(4))
COLLECT = tuple((b, a) for a, b in SPREAD)
SMALL = pltpu.CompilerParams(vmem_limit_bytes=10 * 1024 * 1024)
LARGE = pltpu.CompilerParams(vmem_limit_bytes=20 * 1024 * 1024)


def decode(block):
    codes = block[:TILE].astype(f32)
    power = block[TILE : TILE + EXTRA].astype(f32)[:1]
    return codes * (jnp.exp2(power - 15.0) * (32768.0 / BIG))


def encode(part, square_sum, out_ref, tile):
    start = tile * (TILE + EXTRA)
    top = jnp.max(jnp.abs(part), axis=0, keepdims=True)
    power = jnp.clip(jnp.floor(jnp.log2(jnp.maximum(top, 1e-30))) + 1.0, -90.0, 90.0)
    codes = part * (jnp.exp2(15.0 - power) * (BIG / 32768.0))
    codes = jnp.clip(jnp.round(codes), -32767.0, 32767.0)
    sum_power = jnp.clip(jnp.floor(jnp.log2(jnp.maximum(square_sum, 1e-30))) + 1.0, -100.0, 100.0)
    scaled = square_sum * jnp.exp2(15.0 - sum_power)
    high = jnp.minimum(jnp.floor(scaled), 32767.0)
    spare = jnp.zeros((EXTRA - 4, part.shape[1]), f32)
    extra = jnp.concatenate([power, sum_power, high, jnp.round((scaled - high) * 16384.0), spare], axis=0)
    out_ref[start : start + TILE] = codes.astype(i32).astype(i16)
    out_ref[start + TILE : start + TILE + EXTRA] = extra.astype(i32).astype(i16)


def decode_sum(block):
    extra = block[TILE : TILE + EXTRA].astype(f32)
    return (extra[2:3] + extra[3:4] * (1.0 / 16384.0)) * jnp.exp2(extra[1:2] - 15.0)


def inside(part, rows, start):
    index = lax.broadcasted_iota(i32, part.shape, 0) + start
    return jnp.where(index < rows, part, 0.0)


def first_kernel(rows, half, head_ref, x_ref, sum_ref, out_ref):
    for tile in range(HALF_TILES):
        at = tile * TILE
        part = jnp.dot(head_ref[at : at + TILE], x_ref[...], preferred_element_type=f32)
        if (half * HALF_TILES + tile + 1) * TILE > rows:
            part = inside(part, rows, (half * HALF_TILES + tile) * TILE)
        encode(part, sum_ref[...], out_ref, tile)


def first_message(head_t, x, square_sum, half):
    rows, feats = head_t.shape
    tokens = x.shape[1]
    block = TILE + EXTRA
    whole = lambda i: (0, 0)
    return pl.pallas_call(
        functools.partial(first_kernel, rows, half),
        out_shape=jax.ShapeDtypeStruct((HALF_TILES * block, tokens), i16),
        grid=(1,),
        in_specs=[
            pl.BlockSpec((HALF_TILES * TILE, feats), lambda i: (half, 0)),
            pl.BlockSpec((feats, tokens), whole),
            pl.BlockSpec((1, tokens), whole),
        ],
        out_specs=pl.BlockSpec((HALF_TILES * block, tokens), whole),
        compiler_params=SMALL,
        cost_estimate=pl.CostEstimate(
            flops=rows * feats * tokens, bytes_accessed=4 * rows * feats, transcendentals=0
        ),
    )(head_t, x, square_sum)


def message_kernel(half, part_ref, sum_ref, arrived_ref, out_ref):
    block = TILE + EXTRA
    for tile in range(HALF_TILES):
        at = (half * HALF_TILES + tile) * TILE
        arrived = arrived_ref[tile * block : (tile + 1) * block]
        encode(part_ref[at : at + TILE] + decode(arrived), sum_ref[...] + decode_sum(arrived), out_ref, tile)


def message(part, square_sum, half, arrived):
    return pl.pallas_call(
        functools.partial(message_kernel, half),
        out_shape=jax.ShapeDtypeStruct(arrived.shape, i16),
        compiler_params=SMALL,
        cost_estimate=pl.CostEstimate(
            flops=8 * arrived.size, bytes_accessed=8 * arrived.size, transcendentals=0
        ),
    )(part, square_sum, arrived)


def base_kernel(rows, head_ref, x_ref, out_ref):
    part = jnp.dot(head_ref[...], x_ref[...], preferred_element_type=f32)
    out_ref[...] = inside(part, rows, pl.program_id(0) * HALF_TILES * TILE)


def base(head_t, x):
    rows, feats = head_t.shape
    tokens = x.shape[1]
    return pl.pallas_call(
        functools.partial(base_kernel, rows),
        out_shape=jax.ShapeDtypeStruct((2 * HALF_TILES * TILE, tokens), f32),
        grid=(2,),
        in_specs=[
            pl.BlockSpec((HALF_TILES * TILE, feats), lambda i: (i, 0)),
            pl.BlockSpec((feats, tokens), lambda i: (0, 0)),
        ],
        out_specs=pl.BlockSpec((HALF_TILES * TILE, tokens), lambda i: (i, 0)),
        compiler_params=LARGE,
        cost_estimate=pl.CostEstimate(
            flops=2 * rows * feats * tokens, bytes_accessed=2 * rows * feats, transcendentals=0
        ),
    )(head_t, x)


def finish_kernel(rows, feats, base_ref, a_ref, b_ref, sum_ref, target_ref, pick_ref, e_ref, mine_ref, stats_ref, logits, exps):
    tokens = base_ref.shape[1]
    block = TILE + EXTRA
    square_sum = sum_ref[...] + decode_sum(a_ref[:block, :])
    inverse = lax.rsqrt(square_sum / feats + NORM_EPSILON)
    top = jnp.full((1, tokens), -1e30, f32)
    for tile in range(2 * HALF_TILES):
        at = tile * TILE
        ref, place = (a_ref, tile) if tile < HALF_TILES else (b_ref, tile - HALF_TILES)
        value = (base_ref[at : at + TILE, :] + decode(ref[place * block : (place + 1) * block, :])) * inverse
        if at + TILE > rows:
            index = lax.broadcasted_iota(i32, value.shape, 0) + at
            value = jnp.where(index < rows, value, -1e30)
        logits[at : at + TILE, :] = value
        top = jnp.maximum(top, jnp.max(value, axis=0, keepdims=True))
    total = jnp.zeros((1, tokens), f32)
    weighted = jnp.zeros((1, tokens), f32)
    target = jnp.zeros((1, tokens), f32)
    place = lax.broadcasted_iota(i32, (TILE, tokens), 0)
    for tile in range(2 * HALF_TILES):
        at = tile * TILE
        value = logits[at : at + TILE, :]
        e = jnp.exp(value - top)
        total += jnp.sum(e, axis=0, keepdims=True)
        weighted += jnp.sum(e * value, axis=0, keepdims=True)
        target += jnp.sum(jnp.where(place == target_ref[...] - at, value, 0.0), axis=0, keepdims=True)
        exps[at : at + TILE, :] = e.astype(bf16)
    spare = exps.shape[0] - 2 * HALF_TILES * TILE
    exps[2 * HALF_TILES * TILE :, :] = jnp.zeros((spare, tokens), bf16)
    stats_ref[...] = jnp.concatenate([top, total, weighted, target, inverse], axis=0)
    mine = lax.dot_general(pick_ref[...], exps[...], (((1,), (1,)), ((), ())), preferred_element_type=f32)
    mine_ref[...] = mine[:, :rows].astype(bf16)
    e_ref[...] = exps[:rows, :]


def finish(rows, feats, total, a, b, square_sum, target, pick):
    tokens = total.shape[1]
    padded = -(-rows // 128) * 128
    return pl.pallas_call(
        functools.partial(finish_kernel, rows, float(feats)),
        out_shape=(
            jax.ShapeDtypeStruct((rows, tokens), bf16),
            jax.ShapeDtypeStruct((CHUNK, rows), bf16),
            jax.ShapeDtypeStruct((5, tokens), f32),
        ),
        scratch_shapes=[pltpu.VMEM((2 * HALF_TILES * TILE, tokens), f32), pltpu.VMEM((padded, tokens), bf16)],
        compiler_params=LARGE,
        cost_estimate=pl.CostEstimate(
            flops=2 * rows * CHUNK * tokens, bytes_accessed=10 * rows * tokens, transcendentals=rows * tokens
        ),
    )(total, a, b, square_sum, target, pick)


def grad_kernel(rows, count, core_ref, r0, r1, r2, r3, factor_ref, head_ref, keep_ref, give_ref, left, prod):
    @pl.when(pl.program_id(0) == 0)
    def _():
        for t, ref in enumerate((r0, r1, r2, r3)):
            at = t * CHUNK
            soft = factor_ref[at : at + count, 0:1]
            hard = factor_ref[at : at + count, 1:2]
            target = factor_ref[at : at + count, 2:3].astype(i32)
            index = lax.broadcasted_iota(i32, (count, rows), 1)
            value = ref[...].astype(f32) * soft + jnp.where(index == target, hard, 0.0)
            left[t * count : (t + 1) * count, :] = value.astype(bf16)

    out = jnp.dot(left[...], head_ref[...], preferred_element_type=f32)
    for t in range(4):
        prod[t * 128 : t * 128 + count, :] = out[t * count : (t + 1) * count]
    core = core_ref[0]
    tile = head_ref.shape[1]
    for z in range(2):
        for ref, side in ((keep_ref, core), (give_ref, 1 - core)):
            at = pl.multiple_of((z * 2 + side) * 128, 128)
            turned = prod[pl.ds(at, 128), :].T
            if count == CHUNK:
                ref[z] = turned[:, :CHUNK].astype(bf16)
            else:
                lane = lax.broadcasted_iota(i32, (SHARE // 2, 128), 1)
                for group in range(tile // SHARE):
                    top = turned[group * SHARE : group * SHARE + SHARE // 2]
                    low = turned[group * SHARE + SHARE // 2 : (group + 1) * SHARE]
                    packed = jnp.where(lane < FEW, top, pltpu.roll(low, FEW, 1))
                    ref[z, group * SHARE // 2 : (group + 1) * SHARE // 2] = packed.astype(bf16)


def grad_product(head_t, rows, factors, core, count):
    cols, feats = head_t.shape
    tile = 640
    packed = count != CHUNK
    height = 2 if packed else 1
    lanes = 128 if packed else CHUNK
    out = jax.ShapeDtypeStruct((2, feats // height, lanes), bf16)
    out_spec = pl.BlockSpec((2, tile // height, lanes), lambda i, c: (0, i, 0))
    return pl.pallas_call(
        functools.partial(grad_kernel, cols, count),
        out_shape=(out, out),
        grid_spec=pltpu.PrefetchScalarGridSpec(
            num_scalar_prefetch=1,
            grid=(feats // tile,),
            in_specs=[
                *[pl.BlockSpec((count, cols), lambda i, c: (0, 0)) for r in rows],
                pl.BlockSpec((4 * CHUNK, factors.shape[1]), lambda i, c: (0, 0)),
                pl.BlockSpec((cols, tile), lambda i, c: (0, i)),
            ],
            out_specs=(out_spec, out_spec),
            scratch_shapes=[pltpu.VMEM((4 * count, cols), bf16), pltpu.VMEM((512, tile), f32)],
        ),
        compiler_params=LARGE,
        cost_estimate=pl.CostEstimate(
            flops=8 * count * cols * feats, bytes_accessed=4 * cols * feats, transcendentals=0
        ),
    )(core.reshape(1), *rows, factors, head_t)


def share(value, axes, count, groups=None):
    copies = jnp.broadcast_to(value[None], (count, *value.shape))
    return lax.all_to_all(copies, axes, 0, 0, tiled=True, axis_index_groups=groups)


def shards(hidden, norm_gain, head, token_ids, entropy_mask, group_ids, old_logp, scores):
    tokens, share_cols = hidden.shape
    feats, vocab_cols = head.shape
    section, dp = lax.axis_index(SECTION), lax.axis_index(DP)
    core, low = section % 2, section // 2
    slice_index = lax.axis_index((SECTION, VOCAB))
    head_t = head.T
    hidden_t = hidden.T.astype(f32)
    gain = norm_gain.astype(f32)[:, None]

    rest = jnp.sum(hidden_t * hidden_t, axis=0, keepdims=True)
    pieces = []
    for _ in range(3):
        pieces.append(lax.reduce_precision(rest, 8, 7))
        rest = rest - pieces[-1]
    own = jnp.concatenate([hidden_t * gain, *pieces, jnp.zeros((5, tokens), f32)]).astype(bf16)
    own = lax.ppermute(own, (SECTION, DP), SPREAD)
    lines = share(own, (SECTION, VOCAB), 8, Z_GROUPS)

    blocks = share(lines, VOCAB, 4, X_GROUPS).reshape(4, 2, 4, share_cols + 8, tokens)
    sums = jnp.sum(blocks[:, :, :, share_cols:].astype(f32), axis=(0, 2, 3))
    blocks = blocks[:, :, :, :share_cols].transpose(1, 2, 0, 3, 4).reshape(2, feats, tokens)

    def send(part):
        return lax.ppermute(part, (SECTION, DP), STEP)

    first, later = blocks[0], blocks[1]
    p1 = send(first_message(head_t, first, sums[:1], 0))
    q1 = send(first_message(head_t, first, sums[:1], 1))
    later_pair = lax.ppermute(later, SECTION, CORE_SWAP)
    first_pair = lax.ppermute(first, SECTION, CORE_SWAP)
    sums, later_pair = lax.optimization_barrier((sums, later_pair))
    sums_pair = lax.ppermute(sums, SECTION, CORE_SWAP)
    is_even = core == 0
    second_sum, last_sum = jnp.where(is_even, sums, sums_pair)[1:], jnp.where(is_even, sums_pair, sums)[1:]
    second, last = jnp.where(is_even, later, later_pair), jnp.where(is_even, later_pair, later)
    part2, part3 = lax.optimization_barrier((base(head_t, second), base(head_t, first_pair)))
    p2 = send(message(part2, second_sum, 0, p1))
    q2 = send(message(part2, second_sum, 1, q1))
    p3 = send(message(part3, sums_pair[:1], 0, p2))
    q3 = message(part3, sums_pair[:1], 1, q2)
    q3 = send(q3)
    local_target = token_ids - slice_index * vocab_cols
    local_target = jnp.where(local_target < vocab_cols, local_target, -1)

    chosen = entropy_mask != 0
    position = jnp.where(chosen, jnp.cumsum(chosen.astype(i32)) - 1, -1)
    count = jnp.sum(chosen.astype(i32))
    slots = jnp.arange(CHUNK, dtype=i32)
    pick0 = position[None, :] == slots[:, None]

    own_part = base(head_t, last)
    exps, mine0, stats = finish(
        vocab_cols, share_cols * 64, own_part, p3, q3, last_sum, local_target[None], pick0.astype(bf16)
    )

    def send_rows(mine):
        from_below = lax.ppermute(mine, DP, UP)
        from_above = lax.ppermute(mine, DP, DOWN)
        return from_above, from_below, mine

    def gather_rows(chunk):
        pick = position[None, :] == (slots + chunk * CHUNK)[:, None]
        mine = lax.dot_general(
            pick.astype(bf16), exps, (((1,), (1,)), ((), ())), preferred_element_type=f32
        ).astype(bf16)
        return pick, send_rows(mine)

    rows0 = send_rows(mine0)

    inverse = stats[4]
    every = share(stats[:4], (SECTION, VOCAB), 64)
    row_top = jnp.max(every[:, 0], axis=0)
    scale = jnp.exp(every[:, 0] - row_top)
    exp_total = jnp.sum(scale * every[:, 1], axis=0)
    weighted = jnp.sum(scale * every[:, 2], axis=0)
    target = jnp.sum(every[:, 3], axis=0)
    log_total = row_top + jnp.log(exp_total)
    mean_logit = weighted / exp_total
    entropy = log_total - mean_logit
    new_logp = target - log_total
    first_group = dp * GPD
    members = (
        group_ids[:, None] == first_group + jnp.arange(GPD, dtype=i32)[None, :]
    ).astype(f32)
    group_sum = jnp.sum(scores[:, None] * members, axis=0)
    group_count = jnp.sum(members, axis=0)
    advantage = scores - jnp.sum(members * (group_sum / group_count)[None], axis=1)
    weight = jnp.clip(jnp.exp(new_logp - old_logp), LOW_CLIP, HIGH_CLIP)
    grad_logp = -entropy_mask.astype(f32) * weight * advantage
    soft = -grad_logp * jnp.exp(stats[0] - row_top) / exp_total

    def chunk_grad(pick, rows):
        values = jnp.stack([soft, grad_logp, token_ids.astype(f32), jnp.broadcast_to(count.astype(f32), soft.shape)])
        picked = jnp.sum(jnp.where(pick[None], values[:, None, :], 0.0), axis=2)
        picked = picked.at[3].set(count.astype(f32))
        from_above, from_below, mine = rows
        picked, from_above, from_below = lax.optimization_barrier((picked, from_above, from_below))
        across = lax.ppermute(jnp.where(core == 0, from_below, from_above), (SECTION, DP), STEP)
        rows = from_below, from_above, across, mine
        factors = share(picked, DP, 4)
        most = jnp.max(factors[:, 3, 0]).astype(i32)
        factors = jnp.stack([lax.dynamic_index_in_dim(factors, (dp + r) % 4, 0, False) for r in REL])
        factors = factors.transpose(0, 2, 1).reshape(4 * CHUNK, 4)
        factors = factors - jnp.array([0, 0, 1, 0], f32) * (slice_index * vocab_cols).astype(f32)

        def reduce_rows(size):
            keep, give = grad_product(head_t, rows, factors, core, size)
            part = (keep.astype(f32) + lax.ppermute(give, SECTION, CORE_SWAP).astype(f32)).astype(bf16)
            part = part.reshape(32, -1, part.shape[-1])
            part = lax.all_to_all(
                part, (SECTION, VOCAB), 0, 0, tiled=True, axis_index_groups=CORE_GROUPS
            )
            part = jnp.sum(part.astype(f32), axis=0)
            if size != CHUNK:
                part = jnp.concatenate([part[:, :size], part[:, size:]], axis=0)
            part = lax.ppermute(part, (SECTION, DP), COLLECT)
            return jnp.dot(part, pick[:size].astype(f32), precision=lax.Precision.HIGHEST)

        grad = lax.cond(most <= FEW, lambda: reduce_rows(FEW), lambda: reduce_rows(CHUNK))
        return grad, most

    grad, most = chunk_grad(pick0, rows0)

    def more(state):
        chunk, total = state
        part, _ = chunk_grad(*gather_rows(chunk))
        return chunk + 1, total + part

    _, grad = lax.while_loop(lambda state: state[0] * CHUNK < most, more, (jnp.ones((), i32), grad))

    inner = grad_logp * (target - mean_logit) / (share_cols * 64)
    unit = hidden_t * inverse
    grad_hidden = inverse * (gain * grad - unit * inner[None])
    return new_logp, entropy, grad_hidden.astype(bf16).T


def solution(mesh):
    in_specs = (
        P("dp", ("section", "vocab")),
        P(("section", "vocab")),
        P("dp", ("section", "vocab")),
        P("dp"),
        P("dp"),
        P("dp"),
        P("dp"),
        P("dp"),
    )
    out_specs = (P("dp"), P("dp"), P("dp", ("section", "vocab")))
    return jax.shard_map(shards, mesh=mesh, in_specs=in_specs, out_specs=out_specs, check_vma=False)
```

```python
import functools

import jax
import jax.numpy as jnp
from jax import lax
from jax.experimental import pallas as pl
from jax.experimental.pallas import tpu as pltpu
from jax.sharding import PartitionSpec as P

NORM_EPSILON = 1e-06
LOW_CLIP = 0.5
HIGH_CLIP = 2.0
GPD = 8
CHUNK = 64
SHARE = 80
TILE = 400
EXTRA = 16
HALF_TILES = 3
BIG = 32000.0
REL = (3, 1, 2, 0)
SECTION, DP, VOCAB = "section", "dp", "vocab"
f32, bf16, i16, i32 = jnp.float32, jnp.bfloat16, jnp.int16, jnp.int32
CORE_SWAP = ((0, 1), (1, 0), (2, 3), (3, 2))
UP = tuple((i, (i + 1) % 4) for i in range(4))
DOWN = tuple((i, (i + 3) % 4) for i in range(4))
X_GROUPS = [[z * 4 + x for x in range(4)] for z in range(4)]
Z_GROUPS = [[(a * 2 + c) * 16 + b * 4 + x for a in range(2) for b in range(4)] for c in range(2) for x in range(4)]
STEP = tuple((s * 4 + d, s * 4 + (d + (3 if s % 2 else 1)) % 4) for s in range(4) for d in range(4))
CORE_GROUPS = [[(z * 2 + c) * 16 + v for z in range(2) for v in range(16)] for c in range(2)]
SPREAD = tuple((d * 4 + (d + REL[s]) % 4, s * 4 + d) for s in range(4) for d in range(4))
COLLECT = tuple((b, a) for a, b in SPREAD)
SMALL = pltpu.CompilerParams(vmem_limit_bytes=10 * 1024 * 1024)
LARGE = pltpu.CompilerParams(vmem_limit_bytes=20 * 1024 * 1024)


def decode(block):
    codes = block[:TILE].astype(f32)
    power = block[TILE : TILE + EXTRA].astype(f32)[:1]
    return codes * (jnp.exp2(power - 15.0) * (32768.0 / BIG))


def encode(part, square_sum, out_ref, tile):
    start = tile * (TILE + EXTRA)
    top = jnp.max(jnp.abs(part), axis=0, keepdims=True)
    power = jnp.clip(jnp.floor(jnp.log2(jnp.maximum(top, 1e-30))) + 1.0, -90.0, 90.0)
    codes = part * (jnp.exp2(15.0 - power) * (BIG / 32768.0))
    codes = jnp.clip(jnp.round(codes), -32767.0, 32767.0)
    sum_power = jnp.clip(jnp.floor(jnp.log2(jnp.maximum(square_sum, 1e-30))) + 1.0, -100.0, 100.0)
    scaled = square_sum * jnp.exp2(15.0 - sum_power)
    high = jnp.minimum(jnp.floor(scaled), 32767.0)
    spare = jnp.zeros((EXTRA - 4, part.shape[1]), f32)
    extra = jnp.concatenate([power, sum_power, high, jnp.round((scaled - high) * 16384.0), spare], axis=0)
    out_ref[start : start + TILE] = codes.astype(i32).astype(i16)
    out_ref[start + TILE : start + TILE + EXTRA] = extra.astype(i32).astype(i16)


def decode_sum(block):
    extra = block[TILE : TILE + EXTRA].astype(f32)
    return (extra[2:3] + extra[3:4] * (1.0 / 16384.0)) * jnp.exp2(extra[1:2] - 15.0)


def inside(part, rows, start):
    index = lax.broadcasted_iota(i32, part.shape, 0) + start
    return jnp.where(index < rows, part, 0.0)


def first_kernel(rows, half, head_ref, x_ref, sum_ref, out_ref):
    for tile in range(HALF_TILES):
        at = tile * TILE
        part = jnp.dot(head_ref[at : at + TILE], x_ref[...], preferred_element_type=f32)
        if (half * HALF_TILES + tile + 1) * TILE > rows:
            part = inside(part, rows, (half * HALF_TILES + tile) * TILE)
        encode(part, sum_ref[...], out_ref, tile)


def first_message(head_t, x, square_sum, half):
    rows, feats = head_t.shape
    tokens = x.shape[1]
    block = TILE + EXTRA
    whole = lambda i: (0, 0)
    return pl.pallas_call(
        functools.partial(first_kernel, rows, half),
        out_shape=jax.ShapeDtypeStruct((HALF_TILES * block, tokens), i16),
        grid=(1,),
        in_specs=[
            pl.BlockSpec((HALF_TILES * TILE, feats), lambda i: (half, 0)),
            pl.BlockSpec((feats, tokens), whole),
            pl.BlockSpec((1, tokens), whole),
        ],
        out_specs=pl.BlockSpec((HALF_TILES * block, tokens), whole),
        compiler_params=SMALL,
        cost_estimate=pl.CostEstimate(
            flops=rows * feats * tokens, bytes_accessed=4 * rows * feats, transcendentals=0
        ),
    )(head_t, x, square_sum)


def message_kernel(half, part_ref, sum_ref, arrived_ref, out_ref):
    block = TILE + EXTRA
    for tile in range(HALF_TILES):
        at = (half * HALF_TILES + tile) * TILE
        arrived = arrived_ref[tile * block : (tile + 1) * block]
        encode(part_ref[at : at + TILE] + decode(arrived), sum_ref[...] + decode_sum(arrived), out_ref, tile)


def message(part, square_sum, half, arrived):
    return pl.pallas_call(
        functools.partial(message_kernel, half),
        out_shape=jax.ShapeDtypeStruct(arrived.shape, i16),
        compiler_params=SMALL,
        cost_estimate=pl.CostEstimate(
            flops=8 * arrived.size, bytes_accessed=8 * arrived.size, transcendentals=0
        ),
    )(part, square_sum, arrived)


def base_kernel(rows, head_ref, x_ref, out_ref):
    part = jnp.dot(head_ref[...], x_ref[...], preferred_element_type=f32)
    out_ref[...] = inside(part, rows, pl.program_id(0) * HALF_TILES * TILE)


def base(head_t, x):
    rows, feats = head_t.shape
    tokens = x.shape[1]
    return pl.pallas_call(
        functools.partial(base_kernel, rows),
        out_shape=jax.ShapeDtypeStruct((2 * HALF_TILES * TILE, tokens), f32),
        grid=(2,),
        in_specs=[
            pl.BlockSpec((HALF_TILES * TILE, feats), lambda i: (i, 0)),
            pl.BlockSpec((feats, tokens), lambda i: (0, 0)),
        ],
        out_specs=pl.BlockSpec((HALF_TILES * TILE, tokens), lambda i: (i, 0)),
        compiler_params=LARGE,
        cost_estimate=pl.CostEstimate(
            flops=2 * rows * feats * tokens, bytes_accessed=2 * rows * feats, transcendentals=0
        ),
    )(head_t, x)


def finish_kernel(rows, feats, base_ref, a_ref, b_ref, sum_ref, target_ref, pick_ref, e_ref, mine_ref, stats_ref, logits, exps):
    tokens = base_ref.shape[1]
    block = TILE + EXTRA
    square_sum = sum_ref[...] + decode_sum(a_ref[:block, :])
    inverse = lax.rsqrt(square_sum / feats + NORM_EPSILON)
    top = jnp.full((1, tokens), -1e30, f32)
    for tile in range(2 * HALF_TILES):
        at = tile * TILE
        ref, place = (a_ref, tile) if tile < HALF_TILES else (b_ref, tile - HALF_TILES)
        value = (base_ref[at : at + TILE, :] + decode(ref[place * block : (place + 1) * block, :])) * inverse
        if at + TILE > rows:
            index = lax.broadcasted_iota(i32, value.shape, 0) + at
            value = jnp.where(index < rows, value, -1e30)
        logits[at : at + TILE, :] = value
        top = jnp.maximum(top, jnp.max(value, axis=0, keepdims=True))
    total = jnp.zeros((1, tokens), f32)
    weighted = jnp.zeros((1, tokens), f32)
    target = jnp.zeros((1, tokens), f32)
    place = lax.broadcasted_iota(i32, (TILE, tokens), 0)
    for tile in range(2 * HALF_TILES):
        at = tile * TILE
        value = logits[at : at + TILE, :]
        e = jnp.exp(value - top)
        total += jnp.sum(e, axis=0, keepdims=True)
        weighted += jnp.sum(e * value, axis=0, keepdims=True)
        target += jnp.sum(jnp.where(place == target_ref[...] - at, value, 0.0), axis=0, keepdims=True)
        exps[at : at + TILE, :] = e.astype(bf16)
    spare = exps.shape[0] - 2 * HALF_TILES * TILE
    exps[2 * HALF_TILES * TILE :, :] = jnp.zeros((spare, tokens), bf16)
    stats_ref[...] = jnp.concatenate([top, total, weighted, target, inverse], axis=0)
    mine = lax.dot_general(pick_ref[...], exps[...], (((1,), (1,)), ((), ())), preferred_element_type=f32)
    mine_ref[...] = mine[:, :rows].astype(bf16)
    e_ref[...] = exps[:rows, :]


def finish(rows, feats, total, a, b, square_sum, target, pick):
    tokens = total.shape[1]
    padded = -(-rows // 128) * 128
    return pl.pallas_call(
        functools.partial(finish_kernel, rows, float(feats)),
        out_shape=(
            jax.ShapeDtypeStruct((rows, tokens), bf16),
            jax.ShapeDtypeStruct((CHUNK, rows), bf16),
            jax.ShapeDtypeStruct((5, tokens), f32),
        ),
        scratch_shapes=[pltpu.VMEM((2 * HALF_TILES * TILE, tokens), f32), pltpu.VMEM((padded, tokens), bf16)],
        compiler_params=LARGE,
        cost_estimate=pl.CostEstimate(
            flops=2 * rows * CHUNK * tokens, bytes_accessed=10 * rows * tokens, transcendentals=rows * tokens
        ),
    )(total, a, b, square_sum, target, pick)


def grad_kernel(rows, core_ref, r0, r1, r2, r3, factor_ref, head_ref, keep_ref, give_ref, left, prod):
    @pl.when(pl.program_id(0) == 0)
    def _():
        for t, ref in enumerate((r0, r1, r2, r3)):
            @pl.loop(0, CHUNK // 16)
            def _(step, t=t, ref=ref):
                here = pl.ds(pl.multiple_of(step * 16, 16), 16)
                factor = factor_ref[pl.ds(pl.multiple_of(t * CHUNK + step * 16, 16), 16), :]
                index = lax.broadcasted_iota(i32, (16, rows), 1)
                hard = jnp.where(index == factor[:, 2:3].astype(i32), factor[:, 1:2], 0.0)
                value = ref[here, :].astype(f32) * factor[:, 0:1] + hard
                left[pl.ds(pl.multiple_of(t * CHUNK + step * 16, 16), 16), :] = value.astype(bf16)

    out = jnp.dot(left[...], head_ref[...], preferred_element_type=f32)
    for t in range(4):
        prod[t * 128 : t * 128 + CHUNK, :] = out[t * CHUNK : (t + 1) * CHUNK]
    core = core_ref[0]
    tile = head_ref.shape[1]
    for z in range(2):
        for ref, side in ((keep_ref, core), (give_ref, 1 - core)):
            at = pl.multiple_of((z * 2 + side) * 128, 128)
            turned = prod[pl.ds(at, 128), :].T
            lane = lax.broadcasted_iota(i32, (SHARE // 2, 128), 1)
            for group in range(tile // SHARE):
                top = turned[group * SHARE : group * SHARE + SHARE // 2]
                low = turned[group * SHARE + SHARE // 2 : (group + 1) * SHARE]
                packed = jnp.where(lane < CHUNK, top, pltpu.roll(low, CHUNK, 1))
                ref[z, group * SHARE // 2 : (group + 1) * SHARE // 2] = packed.astype(bf16)


def grad_product(head_t, rows, factors, core):
    cols, feats = head_t.shape
    tile = 640
    out = jax.ShapeDtypeStruct((2, feats // 2, 128), bf16)
    out_spec = pl.BlockSpec((2, tile // 2, 128), lambda i, c: (0, i, 0))
    return pl.pallas_call(
        functools.partial(grad_kernel, cols),
        out_shape=(out, out),
        grid_spec=pltpu.PrefetchScalarGridSpec(
            num_scalar_prefetch=1,
            grid=(feats // tile,),
            in_specs=[
                *[pl.BlockSpec((CHUNK, cols), lambda i, c: (0, 0)) for r in rows],
                pl.BlockSpec((4 * CHUNK, factors.shape[1]), lambda i, c: (0, 0)),
                pl.BlockSpec((cols, tile), lambda i, c: (0, i)),
            ],
            out_specs=(out_spec, out_spec),
            scratch_shapes=[pltpu.VMEM((4 * CHUNK, cols), bf16), pltpu.VMEM((512, tile), f32)],
        ),
        compiler_params=LARGE,
        cost_estimate=pl.CostEstimate(
            flops=8 * CHUNK * cols * feats, bytes_accessed=4 * cols * feats, transcendentals=0
        ),
    )(core.reshape(1), *rows, factors, head_t)


def share(value, axes, count, groups=None):
    copies = jnp.broadcast_to(value[None], (count, *value.shape))
    return lax.all_to_all(copies, axes, 0, 0, tiled=True, axis_index_groups=groups)


def shards(hidden, norm_gain, head, token_ids, entropy_mask, group_ids, old_logp, scores):
    tokens, share_cols = hidden.shape
    feats, vocab_cols = head.shape
    section, dp = lax.axis_index(SECTION), lax.axis_index(DP)
    core, low = section % 2, section // 2
    slice_index = lax.axis_index((SECTION, VOCAB))
    head_t = head.T
    hidden_t = hidden.T.astype(f32)
    gain = norm_gain.astype(f32)[:, None]

    rest = jnp.sum(hidden_t * hidden_t, axis=0, keepdims=True)
    pieces = []
    for _ in range(3):
        pieces.append(lax.reduce_precision(rest, 8, 7))
        rest = rest - pieces[-1]
    own = jnp.concatenate([hidden_t * gain, *pieces, jnp.zeros((5, tokens), f32)]).astype(bf16)
    own = lax.ppermute(own, (SECTION, DP), SPREAD)
    lines = share(own, (SECTION, VOCAB), 8, Z_GROUPS)

    blocks = share(lines, VOCAB, 4, X_GROUPS).reshape(4, 2, 4, share_cols + 8, tokens)
    sums = jnp.sum(blocks[:, :, :, share_cols:].astype(f32), axis=(0, 2, 3))
    blocks = blocks[:, :, :, :share_cols].transpose(1, 2, 0, 3, 4).reshape(2, feats, tokens)

    def send(part):
        return lax.ppermute(part, (SECTION, DP), STEP)

    first, later = blocks[0], blocks[1]
    p1 = send(first_message(head_t, first, sums[:1], 0))
    q1 = send(first_message(head_t, first, sums[:1], 1))
    later_pair = lax.ppermute(later, SECTION, CORE_SWAP)
    first_pair = lax.ppermute(first, SECTION, CORE_SWAP)
    sums, later_pair = lax.optimization_barrier((sums, later_pair))
    sums_pair = lax.ppermute(sums, SECTION, CORE_SWAP)
    is_even = core == 0
    second_sum, last_sum = jnp.where(is_even, sums, sums_pair)[1:], jnp.where(is_even, sums_pair, sums)[1:]
    second, last = jnp.where(is_even, later, later_pair), jnp.where(is_even, later_pair, later)
    part2, part3 = lax.optimization_barrier((base(head_t, second), base(head_t, first_pair)))
    p2 = send(message(part2, second_sum, 0, p1))
    q2 = send(message(part2, second_sum, 1, q1))
    p3 = send(message(part3, sums_pair[:1], 0, p2))
    q3 = message(part3, sums_pair[:1], 1, q2)
    q3 = send(q3)
    local_target = token_ids - slice_index * vocab_cols
    local_target = jnp.where(local_target < vocab_cols, local_target, -1)

    chosen = entropy_mask != 0
    position = jnp.where(chosen, jnp.cumsum(chosen.astype(i32)) - 1, -1)
    count = jnp.sum(chosen.astype(i32))
    slots = jnp.arange(CHUNK, dtype=i32)
    pick0 = position[None, :] == slots[:, None]

    own_part = base(head_t, last)
    exps, mine0, stats = finish(
        vocab_cols, share_cols * 64, own_part, p3, q3, last_sum, local_target[None], pick0.astype(bf16)
    )

    def send_rows(mine):
        from_below = lax.ppermute(mine, DP, UP)
        from_above = lax.ppermute(mine, DP, DOWN)
        return from_above, from_below, mine

    def gather_rows(chunk):
        pick = position[None, :] == (slots + chunk * CHUNK)[:, None]
        mine = lax.dot_general(
            pick.astype(bf16), exps, (((1,), (1,)), ((), ())), preferred_element_type=f32
        ).astype(bf16)
        return pick, send_rows(mine)

    rows0 = send_rows(mine0)

    inverse = stats[4]
    every = share(stats[:4], (SECTION, VOCAB), 64)
    row_top = jnp.max(every[:, 0], axis=0)
    scale = jnp.exp(every[:, 0] - row_top)
    exp_total = jnp.sum(scale * every[:, 1], axis=0)
    weighted = jnp.sum(scale * every[:, 2], axis=0)
    target = jnp.sum(every[:, 3], axis=0)
    log_total = row_top + jnp.log(exp_total)
    mean_logit = weighted / exp_total
    entropy = log_total - mean_logit
    new_logp = target - log_total
    first_group = dp * GPD
    members = (
        group_ids[:, None] == first_group + jnp.arange(GPD, dtype=i32)[None, :]
    ).astype(f32)
    group_sum = jnp.sum(scores[:, None] * members, axis=0)
    group_count = jnp.sum(members, axis=0)
    advantage = scores - jnp.sum(members * (group_sum / group_count)[None], axis=1)
    weight = jnp.clip(jnp.exp(new_logp - old_logp), LOW_CLIP, HIGH_CLIP)
    grad_logp = -entropy_mask.astype(f32) * weight * advantage
    soft = -grad_logp * jnp.exp(stats[0] - row_top) / exp_total

    def chunk_grad(pick, rows):
        values = jnp.stack([soft, grad_logp, token_ids.astype(f32), jnp.broadcast_to(count.astype(f32), soft.shape)])
        picked = jnp.sum(jnp.where(pick[None], values[:, None, :], 0.0), axis=2)
        picked = picked.at[3].set(count.astype(f32))
        from_above, from_below, mine = rows
        picked, from_above, from_below = lax.optimization_barrier((picked, from_above, from_below))
        across = lax.ppermute(jnp.where(core == 0, from_below, from_above), (SECTION, DP), STEP)
        rows = from_below, from_above, across, mine
        factors = share(picked, DP, 4)
        most = jnp.max(factors[:, 3, 0]).astype(i32)
        factors = jnp.stack([lax.dynamic_index_in_dim(factors, (dp + r) % 4, 0, False) for r in REL])
        factors = factors.transpose(0, 2, 1).reshape(4 * CHUNK, 4)
        factors = factors - jnp.array([0, 0, 1, 0], f32) * (slice_index * vocab_cols).astype(f32)

        keep, give = grad_product(head_t, rows, factors, core)
        part = (keep.astype(f32) + lax.ppermute(give, SECTION, CORE_SWAP).astype(f32)).astype(bf16)
        part = part.reshape(32, -1, part.shape[-1])
        part = lax.all_to_all(
            part, (SECTION, VOCAB), 0, 0, tiled=True, axis_index_groups=CORE_GROUPS
        )
        part = jnp.sum(part.astype(f32), axis=0)
        part = jnp.concatenate([part[:, :CHUNK], part[:, CHUNK:]], axis=0)
        part = lax.ppermute(part, (SECTION, DP), COLLECT)
        return jnp.dot(part, pick.astype(f32), precision=lax.Precision.HIGHEST), most

    grad, most = chunk_grad(pick0, rows0)

    def more(state):
        chunk, total = state
        part, _ = chunk_grad(*gather_rows(chunk))
        return chunk + 1, total + part

    _, grad = lax.while_loop(lambda state: state[0] * CHUNK < most, more, (jnp.ones((), i32), grad))

    inner = grad_logp * (target - mean_logit) / (share_cols * 64)
    unit = hidden_t * inverse
    grad_hidden = inverse * (gain * grad - unit * inner[None])
    return new_logp, entropy, grad_hidden.astype(bf16).T


def solution(mesh):
    in_specs = (
        P("dp", ("section", "vocab")),
        P(("section", "vocab")),
        P("dp", ("section", "vocab")),
        P("dp"),
        P("dp"),
        P("dp"),
        P("dp"),
        P("dp"),
    )
    out_specs = (P("dp"), P("dp"), P("dp", ("section", "vocab")))
    return jax.shard_map(shards, mesh=mesh, in_specs=in_specs, out_specs=out_specs, check_vma=False)
```

```python
import functools

import jax
import jax.numpy as jnp
from jax import lax
from jax.experimental import pallas as pl
from jax.experimental.pallas import tpu as pltpu
from jax.sharding import PartitionSpec as P

NORM_EPSILON = 1e-06
LOW_CLIP = 0.5
HIGH_CLIP = 2.0
GPD = 8
CHUNK = 64
SHARE = 80
TILE = 1200
EXTRA = 16
HALF_TILES = 1
BIG = 32000.0
REL = (3, 1, 2, 0)
SECTION, DP, VOCAB = "section", "dp", "vocab"
f32, bf16, i16, i32 = jnp.float32, jnp.bfloat16, jnp.int16, jnp.int32
CORE_SWAP = ((0, 1), (1, 0), (2, 3), (3, 2))
UP = tuple((i, (i + 1) % 4) for i in range(4))
DOWN = tuple((i, (i + 3) % 4) for i in range(4))
X_GROUPS = [[z * 4 + x for x in range(4)] for z in range(4)]
Z_GROUPS = [[(a * 2 + c) * 16 + b * 4 + x for a in range(2) for b in range(4)] for c in range(2) for x in range(4)]
STEP = tuple((s * 4 + d, s * 4 + (d + (3 if s % 2 else 1)) % 4) for s in range(4) for d in range(4))
CORE_GROUPS = [[(z * 2 + c) * 16 + v for z in range(2) for v in range(16)] for c in range(2)]
SPREAD = tuple((d * 4 + (d + REL[s]) % 4, s * 4 + d) for s in range(4) for d in range(4))
COLLECT = tuple((b, a) for a, b in SPREAD)
SMALL = pltpu.CompilerParams(vmem_limit_bytes=10 * 1024 * 1024)
LARGE = pltpu.CompilerParams(vmem_limit_bytes=15 * 1024 * 1024)


def decode(block):
    codes = block[:TILE].astype(f32)
    power = block[TILE : TILE + EXTRA].astype(f32)[:1]
    return codes * (jnp.exp2(power - 15.0) * (32768.0 / BIG))


def encode(part, square_sum, out_ref, tile):
    start = tile * (TILE + EXTRA)
    top = jnp.max(jnp.abs(part), axis=0, keepdims=True)
    power = jnp.clip(jnp.floor(jnp.log2(jnp.maximum(top, 1e-30))) + 1.0, -90.0, 90.0)
    codes = part * (jnp.exp2(15.0 - power) * (BIG / 32768.0))
    codes = jnp.clip(jnp.round(codes), -32767.0, 32767.0)
    sum_power = jnp.clip(jnp.floor(jnp.log2(jnp.maximum(square_sum, 1e-30))) + 1.0, -100.0, 100.0)
    scaled = square_sum * jnp.exp2(15.0 - sum_power)
    high = jnp.minimum(jnp.floor(scaled), 32767.0)
    spare = jnp.zeros((EXTRA - 4, part.shape[1]), f32)
    extra = jnp.concatenate([power, sum_power, high, jnp.round((scaled - high) * 16384.0), spare], axis=0)
    out_ref[start : start + TILE] = codes.astype(i32).astype(i16)
    out_ref[start + TILE : start + TILE + EXTRA] = extra.astype(i32).astype(i16)


def decode_sum(block):
    extra = block[TILE : TILE + EXTRA].astype(f32)
    return (extra[2:3] + extra[3:4] * (1.0 / 16384.0)) * jnp.exp2(extra[1:2] - 15.0)


def inside(part, rows, start):
    index = lax.broadcasted_iota(i32, part.shape, 0) + start
    return jnp.where(index < rows, part, 0.0)


def first_kernel(rows, half, head_ref, x_ref, sum_ref, out_ref):
    for tile in range(HALF_TILES):
        at = tile * TILE
        part = jnp.dot(head_ref[at : at + TILE], x_ref[...], preferred_element_type=f32)
        if (half * HALF_TILES + tile + 1) * TILE > rows:
            part = inside(part, rows, (half * HALF_TILES + tile) * TILE)
        encode(part, sum_ref[...], out_ref, tile)


def first_message(head_t, x, square_sum, half):
    rows, feats = head_t.shape
    tokens = x.shape[1]
    block = TILE + EXTRA
    whole = lambda i: (0, 0)
    return pl.pallas_call(
        functools.partial(first_kernel, rows, half),
        out_shape=jax.ShapeDtypeStruct((HALF_TILES * block, tokens), i16),
        grid=(1,),
        in_specs=[
            pl.BlockSpec((HALF_TILES * TILE, feats), lambda i: (half, 0)),
            pl.BlockSpec((feats, tokens), whole),
            pl.BlockSpec((1, tokens), whole),
        ],
        out_specs=pl.BlockSpec((HALF_TILES * block, tokens), whole),
        compiler_params=SMALL,
        cost_estimate=pl.CostEstimate(
            flops=rows * feats * tokens, bytes_accessed=4 * rows * feats, transcendentals=0
        ),
    )(head_t, x, square_sum)


def message_kernel(half, part_ref, sum_ref, arrived_ref, out_ref):
    block = TILE + EXTRA
    for tile in range(HALF_TILES):
        at = (half * HALF_TILES + tile) * TILE
        arrived = arrived_ref[tile * block : (tile + 1) * block]
        encode(part_ref[at : at + TILE] + decode(arrived), sum_ref[...] + decode_sum(arrived), out_ref, tile)


def message(part, square_sum, half, arrived):
    return pl.pallas_call(
        functools.partial(message_kernel, half),
        out_shape=jax.ShapeDtypeStruct(arrived.shape, i16),
        compiler_params=SMALL,
        cost_estimate=pl.CostEstimate(
            flops=8 * arrived.size, bytes_accessed=8 * arrived.size, transcendentals=0
        ),
    )(part, square_sum, arrived)


def base_kernel(rows, head_ref, x_ref, out_ref):
    part = jnp.dot(head_ref[...], x_ref[...], preferred_element_type=f32)
    out_ref[...] = inside(part, rows, pl.program_id(0) * HALF_TILES * TILE)


def base(head_t, x):
    rows, feats = head_t.shape
    tokens = x.shape[1]
    return pl.pallas_call(
        functools.partial(base_kernel, rows),
        out_shape=jax.ShapeDtypeStruct((2 * HALF_TILES * TILE, tokens), f32),
        grid=(2,),
        in_specs=[
            pl.BlockSpec((HALF_TILES * TILE, feats), lambda i: (i, 0)),
            pl.BlockSpec((feats, tokens), lambda i: (0, 0)),
        ],
        out_specs=pl.BlockSpec((HALF_TILES * TILE, tokens), lambda i: (i, 0)),
        compiler_params=LARGE,
        cost_estimate=pl.CostEstimate(
            flops=2 * rows * feats * tokens, bytes_accessed=2 * rows * feats, transcendentals=0
        ),
    )(head_t, x)


def finish_kernel(rows, feats, base_ref, a_ref, b_ref, sum_ref, target_ref, pick_ref, e_ref, mine_ref, stats_ref, logits, exps):
    tokens = base_ref.shape[1]
    block = TILE + EXTRA
    square_sum = sum_ref[...] + decode_sum(a_ref[:block, :])
    inverse = lax.rsqrt(square_sum / feats + NORM_EPSILON)
    top = jnp.full((1, tokens), -1e30, f32)
    for tile in range(2 * HALF_TILES):
        at = tile * TILE
        ref, place = (a_ref, tile) if tile < HALF_TILES else (b_ref, tile - HALF_TILES)
        value = (base_ref[at : at + TILE, :] + decode(ref[place * block : (place + 1) * block, :])) * inverse
        if at + TILE > rows:
            index = lax.broadcasted_iota(i32, value.shape, 0) + at
            value = jnp.where(index < rows, value, -1e30)
        logits[at : at + TILE, :] = value
        top = jnp.maximum(top, jnp.max(value, axis=0, keepdims=True))
    total = jnp.zeros((1, tokens), f32)
    weighted = jnp.zeros((1, tokens), f32)
    target = jnp.zeros((1, tokens), f32)
    place = lax.broadcasted_iota(i32, (TILE, tokens), 0)
    for tile in range(2 * HALF_TILES):
        at = tile * TILE
        value = logits[at : at + TILE, :]
        e = jnp.exp(value - top)
        total += jnp.sum(e, axis=0, keepdims=True)
        weighted += jnp.sum(e * value, axis=0, keepdims=True)
        target += jnp.sum(jnp.where(place == target_ref[...] - at, value, 0.0), axis=0, keepdims=True)
        exps[at : at + TILE, :] = e.astype(bf16)
    spare = exps.shape[0] - 2 * HALF_TILES * TILE
    exps[2 * HALF_TILES * TILE :, :] = jnp.zeros((spare, tokens), bf16)
    stats_ref[...] = jnp.concatenate([top, total, weighted, target, inverse], axis=0)
    mine = lax.dot_general(pick_ref[...], exps[...], (((1,), (1,)), ((), ())), preferred_element_type=f32)
    mine_ref[...] = mine[:, :rows].astype(bf16)
    e_ref[...] = exps[:rows, :]


def finish(rows, feats, total, a, b, square_sum, target, pick):
    tokens = total.shape[1]
    padded = -(-rows // 128) * 128
    return pl.pallas_call(
        functools.partial(finish_kernel, rows, float(feats)),
        out_shape=(
            jax.ShapeDtypeStruct((rows, tokens), bf16),
            jax.ShapeDtypeStruct((CHUNK, rows), bf16),
            jax.ShapeDtypeStruct((5, tokens), f32),
        ),
        scratch_shapes=[pltpu.VMEM((2 * HALF_TILES * TILE, tokens), f32), pltpu.VMEM((padded, tokens), bf16)],
        compiler_params=LARGE,
        cost_estimate=pl.CostEstimate(
            flops=2 * rows * CHUNK * tokens, bytes_accessed=10 * rows * tokens, transcendentals=rows * tokens
        ),
    )(total, a, b, square_sum, target, pick)


def grad_kernel(rows, core_ref, r0, r1, r2, r3, factor_ref, head_ref, keep_ref, give_ref, left, prod):
    @pl.when(pl.program_id(0) == 0)
    def _():
        for t, ref in enumerate((r0, r1, r2, r3)):
            factor = factor_ref[t * CHUNK : (t + 1) * CHUNK, :]
            index = lax.broadcasted_iota(i32, (CHUNK, rows), 1)
            hard = jnp.where(index == factor[:, 2:3].astype(i32), factor[:, 1:2], 0.0)
            value = ref[...].astype(f32) * factor[:, 0:1] + hard
            left[t * CHUNK : (t + 1) * CHUNK, :] = value.astype(bf16)

    out = jnp.dot(left[...], head_ref[...], preferred_element_type=f32)
    for t in range(4):
        prod[t * 128 : t * 128 + CHUNK, :] = out[t * CHUNK : (t + 1) * CHUNK]
    core = core_ref[0]
    tile = head_ref.shape[1]
    for z in range(2):
        for ref, side in ((keep_ref, core), (give_ref, 1 - core)):
            at = pl.multiple_of((z * 2 + side) * 128, 128)
            turned = prod[pl.ds(at, 128), :].T
            lane = lax.broadcasted_iota(i32, (SHARE // 2, 128), 1)
            for group in range(tile // SHARE):
                top = turned[group * SHARE : group * SHARE + SHARE // 2]
                low = turned[group * SHARE + SHARE // 2 : (group + 1) * SHARE]
                packed = jnp.where(lane < CHUNK, top, pltpu.roll(low, CHUNK, 1))
                ref[z, group * SHARE // 2 : (group + 1) * SHARE // 2] = packed.astype(bf16)


def grad_product(head_t, rows, factors, core):
    cols, feats = head_t.shape
    tile = 640
    out = jax.ShapeDtypeStruct((2, feats // 2, 128), bf16)
    out_spec = pl.BlockSpec((2, tile // 2, 128), lambda i, c: (0, i, 0))
    return pl.pallas_call(
        functools.partial(grad_kernel, cols),
        out_shape=(out, out),
        grid_spec=pltpu.PrefetchScalarGridSpec(
            num_scalar_prefetch=1,
            grid=(feats // tile,),
            in_specs=[
                *[pl.BlockSpec((CHUNK, cols), lambda i, c: (0, 0)) for r in rows],
                pl.BlockSpec((4 * CHUNK, factors.shape[1]), lambda i, c: (0, 0)),
                pl.BlockSpec((cols, tile), lambda i, c: (0, i)),
            ],
            out_specs=(out_spec, out_spec),
            scratch_shapes=[pltpu.VMEM((4 * CHUNK, cols), bf16), pltpu.VMEM((512, tile), f32)],
        ),
        compiler_params=LARGE,
        cost_estimate=pl.CostEstimate(
            flops=8 * CHUNK * cols * feats, bytes_accessed=4 * cols * feats, transcendentals=0
        ),
    )(core.reshape(1), *rows, factors, head_t)


def share(value, axes, count, groups=None):
    copies = jnp.broadcast_to(value[None], (count, *value.shape))
    return lax.all_to_all(copies, axes, 0, 0, tiled=True, axis_index_groups=groups)


def shards(hidden, norm_gain, head, token_ids, entropy_mask, group_ids, old_logp, scores):
    tokens, share_cols = hidden.shape
    feats, vocab_cols = head.shape
    section, dp = lax.axis_index(SECTION), lax.axis_index(DP)
    core, low = section % 2, section // 2
    slice_index = lax.axis_index((SECTION, VOCAB))
    head_t = head.T
    hidden_t = hidden.T.astype(f32)
    gain = norm_gain.astype(f32)[:, None]

    rest = jnp.sum(hidden_t * hidden_t, axis=0, keepdims=True)
    pieces = []
    for _ in range(3):
        pieces.append(lax.reduce_precision(rest, 8, 7))
        rest = rest - pieces[-1]
    own = jnp.concatenate([hidden_t * gain, *pieces, jnp.zeros((5, tokens), f32)]).astype(bf16)
    own = lax.ppermute(own, (SECTION, DP), SPREAD)
    lines = share(own, (SECTION, VOCAB), 8, Z_GROUPS)

    blocks = share(lines, VOCAB, 4, X_GROUPS).reshape(4, 2, 4, share_cols + 8, tokens)
    sums = jnp.sum(blocks[:, :, :, share_cols:].astype(f32), axis=(0, 2, 3))
    blocks = blocks[:, :, :, :share_cols].transpose(1, 2, 0, 3, 4).reshape(2, feats, tokens)

    def send(part):
        return lax.ppermute(part, (SECTION, DP), STEP)

    first, later = blocks[0], blocks[1]
    p1 = send(first_message(head_t, first, sums[:1], 0))
    q1 = send(first_message(head_t, first, sums[:1], 1))
    later_pair = lax.ppermute(later, SECTION, CORE_SWAP)
    first_pair = lax.ppermute(first, SECTION, CORE_SWAP)
    sums, later_pair = lax.optimization_barrier((sums, later_pair))
    sums_pair = lax.ppermute(sums, SECTION, CORE_SWAP)
    is_even = core == 0
    second_sum, last_sum = jnp.where(is_even, sums, sums_pair)[1:], jnp.where(is_even, sums_pair, sums)[1:]
    second, last = jnp.where(is_even, later, later_pair), jnp.where(is_even, later_pair, later)
    part2, part3 = lax.optimization_barrier((base(head_t, second), base(head_t, first_pair)))
    p2 = send(message(part2, second_sum, 0, p1))
    q2 = send(message(part2, second_sum, 1, q1))
    p3 = send(message(part3, sums_pair[:1], 0, p2))
    q3 = message(part3, sums_pair[:1], 1, q2)
    q3 = send(q3)
    local_target = token_ids - slice_index * vocab_cols
    local_target = jnp.where(local_target < vocab_cols, local_target, -1)

    chosen = entropy_mask != 0
    position = jnp.where(chosen, jnp.cumsum(chosen.astype(i32)) - 1, -1)
    count = jnp.sum(chosen.astype(i32))
    slots = jnp.arange(CHUNK, dtype=i32)
    pick0 = position[None, :] == slots[:, None]

    own_part = base(head_t, last)
    exps, mine0, stats = finish(
        vocab_cols, share_cols * 64, own_part, p3, q3, last_sum, local_target[None], pick0.astype(bf16)
    )

    def send_rows(mine):
        from_below = lax.ppermute(mine, DP, UP)
        from_above = lax.ppermute(mine, DP, DOWN)
        return from_above, from_below, mine

    def gather_rows(chunk):
        pick = position[None, :] == (slots + chunk * CHUNK)[:, None]
        mine = lax.dot_general(
            pick.astype(bf16), exps, (((1,), (1,)), ((), ())), preferred_element_type=f32
        ).astype(bf16)
        return pick, send_rows(mine)

    rows0 = send_rows(mine0)

    inverse = stats[4]
    every = share(stats[:4], (SECTION, VOCAB), 64)
    row_top = jnp.max(every[:, 0], axis=0)
    scale = jnp.exp(every[:, 0] - row_top)
    exp_total = jnp.sum(scale * every[:, 1], axis=0)
    weighted = jnp.sum(scale * every[:, 2], axis=0)
    target = jnp.sum(every[:, 3], axis=0)
    log_total = row_top + jnp.log(exp_total)
    mean_logit = weighted / exp_total
    entropy = log_total - mean_logit
    new_logp = target - log_total
    first_group = dp * GPD
    members = (
        group_ids[:, None] == first_group + jnp.arange(GPD, dtype=i32)[None, :]
    ).astype(f32)
    group_sum = jnp.sum(scores[:, None] * members, axis=0)
    group_count = jnp.sum(members, axis=0)
    advantage = scores - jnp.sum(members * (group_sum / group_count)[None], axis=1)
    weight = jnp.clip(jnp.exp(new_logp - old_logp), LOW_CLIP, HIGH_CLIP)
    grad_logp = -entropy_mask.astype(f32) * weight * advantage
    soft = -grad_logp * jnp.exp(stats[0] - row_top) / exp_total

    def chunk_grad(pick, rows):
        values = jnp.stack([soft, grad_logp, token_ids.astype(f32), jnp.broadcast_to(count.astype(f32), soft.shape)])
        picked = jnp.sum(jnp.where(pick[None], values[:, None, :], 0.0), axis=2)
        picked = picked.at[3].set(count.astype(f32))
        from_above, from_below, mine = rows
        picked, from_above, from_below = lax.optimization_barrier((picked, from_above, from_below))
        across = lax.ppermute(jnp.where(core == 0, from_below, from_above), (SECTION, DP), STEP)
        rows = from_below, from_above, across, mine
        factors = share(picked, DP, 4)
        most = jnp.max(factors[:, 3, 0]).astype(i32)
        factors = jnp.stack([lax.dynamic_index_in_dim(factors, (dp + r) % 4, 0, False) for r in REL])
        factors = factors.transpose(0, 2, 1).reshape(4 * CHUNK, 4)
        factors = factors - jnp.array([0, 0, 1, 0], f32) * (slice_index * vocab_cols).astype(f32)

        keep, give = grad_product(head_t, rows, factors, core)
        part = (keep.astype(f32) + lax.ppermute(give, SECTION, CORE_SWAP).astype(f32)).astype(bf16)
        part = part.reshape(32, -1, part.shape[-1])
        part = lax.all_to_all(
            part, (SECTION, VOCAB), 0, 0, tiled=True, axis_index_groups=CORE_GROUPS
        )
        part = jnp.sum(part.astype(f32), axis=0)
        part = jnp.concatenate([part[:, :CHUNK], part[:, CHUNK:]], axis=0)
        part = lax.ppermute(part, (SECTION, DP), COLLECT)
        return jnp.dot(part, pick.astype(f32), precision=lax.Precision.HIGHEST), most

    grad, most = chunk_grad(pick0, rows0)

    def more(state):
        chunk, total = state
        part, _ = chunk_grad(*gather_rows(chunk))
        return chunk + 1, total + part

    _, grad = lax.while_loop(lambda state: state[0] * CHUNK < most, more, (jnp.ones((), i32), grad))

    inner = grad_logp * (target - mean_logit) / (share_cols * 64)
    unit = hidden_t * inverse
    grad_hidden = inverse * (gain * grad - unit * inner[None])
    return new_logp, entropy, grad_hidden.astype(bf16).T


def solution(mesh):
    in_specs = (
        P("dp", ("section", "vocab")),
        P(("section", "vocab")),
        P("dp", ("section", "vocab")),
        P("dp"),
        P("dp"),
        P("dp"),
        P("dp"),
        P("dp"),
    )
    out_specs = (P("dp"), P("dp"), P("dp", ("section", "vocab")))
    return jax.shard_map(shards, mesh=mesh, in_specs=in_specs, out_specs=out_specs, check_vma=False)
```

```python
import functools

import jax
import jax.numpy as jnp
from jax import lax
from jax.experimental import pallas as pl
from jax.experimental.pallas import tpu as pltpu
from jax.sharding import PartitionSpec as P

NORM_EPSILON = 1e-06
LOW_CLIP = 0.5
HIGH_CLIP = 2.0
GPD = 8
CHUNK = 64
SHARE = 80
TILE = 1200
EXTRA = 16
HALF_TILES = 1
BIG = 32000.0
REL = (3, 1, 2, 0)
SECTION, DP, VOCAB = "section", "dp", "vocab"
f32, bf16, i16, i32 = jnp.float32, jnp.bfloat16, jnp.int16, jnp.int32
CORE_SWAP = ((0, 1), (1, 0), (2, 3), (3, 2))
UP = tuple((i, (i + 1) % 4) for i in range(4))
DOWN = tuple((i, (i + 3) % 4) for i in range(4))
X_GROUPS = [[z * 4 + x for x in range(4)] for z in range(4)]
Z_GROUPS = [[(a * 2 + c) * 16 + b * 4 + x for a in range(2) for b in range(4)] for c in range(2) for x in range(4)]
STEP = tuple((s * 4 + d, s * 4 + (d + (3 if s % 2 else 1)) % 4) for s in range(4) for d in range(4))
CORE_GROUPS = [[(z * 2 + c) * 16 + v for z in range(2) for v in range(16)] for c in range(2)]
SPREAD = tuple((d * 4 + (d + REL[s]) % 4, s * 4 + d) for s in range(4) for d in range(4))
COLLECT = tuple((b, a) for a, b in SPREAD)
SMALL = pltpu.CompilerParams(vmem_limit_bytes=10 * 1024 * 1024)
LARGE = pltpu.CompilerParams(vmem_limit_bytes=15 * 1024 * 1024)


def decode(block):
    codes = block[:TILE].astype(f32)
    power = block[TILE : TILE + EXTRA].astype(f32)[:1]
    return codes * (jnp.exp2(power - 15.0) * (32768.0 / BIG))


def encode(part, square_sum, out_ref, tile):
    start = tile * (TILE + EXTRA)
    top = jnp.max(jnp.abs(part), axis=0, keepdims=True)
    power = jnp.clip(jnp.floor(jnp.log2(jnp.maximum(top, 1e-30))) + 1.0, -90.0, 90.0)
    codes = part * (jnp.exp2(15.0 - power) * (BIG / 32768.0))
    codes = jnp.clip(jnp.round(codes), -32767.0, 32767.0)
    sum_power = jnp.clip(jnp.floor(jnp.log2(jnp.maximum(square_sum, 1e-30))) + 1.0, -100.0, 100.0)
    scaled = square_sum * jnp.exp2(15.0 - sum_power)
    high = jnp.minimum(jnp.floor(scaled), 32767.0)
    spare = jnp.zeros((EXTRA - 4, part.shape[1]), f32)
    extra = jnp.concatenate([power, sum_power, high, jnp.round((scaled - high) * 16384.0), spare], axis=0)
    out_ref[start : start + TILE] = codes.astype(i32).astype(i16)
    out_ref[start + TILE : start + TILE + EXTRA] = extra.astype(i32).astype(i16)


def decode_sum(block):
    extra = block[TILE : TILE + EXTRA].astype(f32)
    return (extra[2:3] + extra[3:4] * (1.0 / 16384.0)) * jnp.exp2(extra[1:2] - 15.0)


def inside(part, rows, start):
    index = lax.broadcasted_iota(i32, part.shape, 0) + start
    return jnp.where(index < rows, part, 0.0)


def first_kernel(rows, half, head_ref, x_ref, sum_ref, out_ref):
    for tile in range(HALF_TILES):
        at = tile * TILE
        part = jnp.dot(head_ref[at : at + TILE], x_ref[...], preferred_element_type=f32)
        if (half * HALF_TILES + tile + 1) * TILE > rows:
            part = inside(part, rows, (half * HALF_TILES + tile) * TILE)
        encode(part, sum_ref[...], out_ref, tile)


def first_message(head_t, x, square_sum, half):
    rows, feats = head_t.shape
    tokens = x.shape[1]
    block = TILE + EXTRA
    whole = lambda i: (0, 0)
    return pl.pallas_call(
        functools.partial(first_kernel, rows, half),
        out_shape=jax.ShapeDtypeStruct((HALF_TILES * block, tokens), i16),
        grid=(1,),
        in_specs=[
            pl.BlockSpec((HALF_TILES * TILE, feats), lambda i: (half, 0)),
            pl.BlockSpec((feats, tokens), whole),
            pl.BlockSpec((1, tokens), whole),
        ],
        out_specs=pl.BlockSpec((HALF_TILES * block, tokens), whole),
        compiler_params=SMALL,
        cost_estimate=pl.CostEstimate(
            flops=rows * feats * tokens, bytes_accessed=4 * rows * feats, transcendentals=0
        ),
    )(head_t, x, square_sum)


def message_kernel(half, part_ref, sum_ref, arrived_ref, out_ref):
    block = TILE + EXTRA
    for tile in range(HALF_TILES):
        at = (half * HALF_TILES + tile) * TILE
        arrived = arrived_ref[tile * block : (tile + 1) * block]
        encode(part_ref[at : at + TILE] + decode(arrived), sum_ref[...] + decode_sum(arrived), out_ref, tile)


def message(part, square_sum, half, arrived):
    return pl.pallas_call(
        functools.partial(message_kernel, half),
        out_shape=jax.ShapeDtypeStruct(arrived.shape, i16),
        compiler_params=SMALL,
        cost_estimate=pl.CostEstimate(
            flops=8 * arrived.size, bytes_accessed=8 * arrived.size, transcendentals=0
        ),
    )(part, square_sum, arrived)


def base_kernel(rows, head_ref, x_ref, out_ref):
    part = jnp.dot(head_ref[...], x_ref[...], preferred_element_type=f32)
    out_ref[...] = inside(part, rows, pl.program_id(0) * HALF_TILES * TILE)


def base(head_t, x):
    rows, feats = head_t.shape
    tokens = x.shape[1]
    return pl.pallas_call(
        functools.partial(base_kernel, rows),
        out_shape=jax.ShapeDtypeStruct((2 * HALF_TILES * TILE, tokens), f32),
        grid=(2,),
        in_specs=[
            pl.BlockSpec((HALF_TILES * TILE, feats), lambda i: (i, 0)),
            pl.BlockSpec((feats, tokens), lambda i: (0, 0)),
        ],
        out_specs=pl.BlockSpec((HALF_TILES * TILE, tokens), lambda i: (i, 0)),
        compiler_params=LARGE,
        cost_estimate=pl.CostEstimate(
            flops=2 * rows * feats * tokens, bytes_accessed=2 * rows * feats, transcendentals=0
        ),
    )(head_t, x)


def finish_kernel(rows, feats, base_ref, a_ref, b_ref, sum_ref, target_ref, pick_ref, e_ref, mine_ref, stats_ref, logits, exps):
    tokens = base_ref.shape[1]
    block = TILE + EXTRA
    square_sum = sum_ref[...] + decode_sum(a_ref[:block, :])
    inverse = lax.rsqrt(square_sum / feats + NORM_EPSILON)
    top = jnp.full((1, tokens), -1e30, f32)
    for tile in range(2 * HALF_TILES):
        at = tile * TILE
        ref, place = (a_ref, tile) if tile < HALF_TILES else (b_ref, tile - HALF_TILES)
        value = (base_ref[at : at + TILE, :] + decode(ref[place * block : (place + 1) * block, :])) * inverse
        if at + TILE > rows:
            index = lax.broadcasted_iota(i32, value.shape, 0) + at
            value = jnp.where(index < rows, value, -1e30)
        logits[at : at + TILE, :] = value
        top = jnp.maximum(top, jnp.max(value, axis=0, keepdims=True))
    total = jnp.zeros((1, tokens), f32)
    weighted = jnp.zeros((1, tokens), f32)
    target = jnp.zeros((1, tokens), f32)
    place = lax.broadcasted_iota(i32, (TILE, tokens), 0)
    for tile in range(2 * HALF_TILES):
        at = tile * TILE
        value = logits[at : at + TILE, :]
        e = jnp.exp(value - top)
        total += jnp.sum(e, axis=0, keepdims=True)
        weighted += jnp.sum(e * value, axis=0, keepdims=True)
        target += jnp.sum(jnp.where(place == target_ref[...] - at, value, 0.0), axis=0, keepdims=True)
        exps[at : at + TILE, :] = e.astype(bf16)
    spare = exps.shape[0] - 2 * HALF_TILES * TILE
    exps[2 * HALF_TILES * TILE :, :] = jnp.zeros((spare, tokens), bf16)
    stats_ref[...] = jnp.concatenate([top, total, weighted, target, inverse], axis=0)
    mine = lax.dot_general(pick_ref[...], exps[...], (((1,), (1,)), ((), ())), preferred_element_type=f32)
    mine_ref[...] = mine[:, :rows].astype(bf16)
    e_ref[...] = exps[:rows, :]


def finish(rows, feats, total, a, b, square_sum, target, pick):
    tokens = total.shape[1]
    padded = -(-rows // 128) * 128
    return pl.pallas_call(
        functools.partial(finish_kernel, rows, float(feats)),
        out_shape=(
            jax.ShapeDtypeStruct((rows, tokens), bf16),
            jax.ShapeDtypeStruct((CHUNK, rows), bf16),
            jax.ShapeDtypeStruct((5, tokens), f32),
        ),
        scratch_shapes=[pltpu.VMEM((2 * HALF_TILES * TILE, tokens), f32), pltpu.VMEM((padded, tokens), bf16)],
        compiler_params=LARGE,
        cost_estimate=pl.CostEstimate(
            flops=2 * rows * CHUNK * tokens, bytes_accessed=10 * rows * tokens, transcendentals=rows * tokens
        ),
    )(total, a, b, square_sum, target, pick)


def grad_kernel(rows, core_ref, r0, r1, r2, r3, factor_ref, head_ref, keep_ref, give_ref, left, prod):
    @pl.when(pl.program_id(0) == 0)
    def _():
        for t, ref in enumerate((r0, r1, r2, r3)):
            factor = factor_ref[t * CHUNK : (t + 1) * CHUNK, :]
            index = lax.broadcasted_iota(i32, (CHUNK, rows), 1)
            hard = jnp.where(index == factor[:, 2:3].astype(i32), factor[:, 1:2], 0.0)
            value = ref[...].astype(f32) * factor[:, 0:1] + hard
            left[t * CHUNK : (t + 1) * CHUNK, :] = value.astype(bf16)

    out = jnp.dot(left[...], head_ref[...], preferred_element_type=f32)
    for t in range(4):
        prod[t * 128 : t * 128 + CHUNK, :] = out[t * CHUNK : (t + 1) * CHUNK]
    core = core_ref[0]
    tile = head_ref.shape[1]
    for z in range(2):
        for ref, side in ((keep_ref, core), (give_ref, 1 - core)):
            at = pl.multiple_of((z * 2 + side) * 128, 128)
            turned = prod[pl.ds(at, 128), :].T
            lane = lax.broadcasted_iota(i32, (SHARE // 2, 128), 1)
            for group in range(tile // SHARE):
                top = turned[group * SHARE : group * SHARE + SHARE // 2]
                low = turned[group * SHARE + SHARE // 2 : (group + 1) * SHARE]
                packed = jnp.where(lane < CHUNK, top, pltpu.roll(low, CHUNK, 1))
                ref[z, group * SHARE // 2 : (group + 1) * SHARE // 2] = packed.astype(bf16)


def grad_product(head_t, rows, factors, core):
    cols, feats = head_t.shape
    tile = 640
    out = jax.ShapeDtypeStruct((2, feats // 2, 128), bf16)
    out_spec = pl.BlockSpec((2, tile // 2, 128), lambda i, c: (0, i, 0))
    return pl.pallas_call(
        functools.partial(grad_kernel, cols),
        out_shape=(out, out),
        grid_spec=pltpu.PrefetchScalarGridSpec(
            num_scalar_prefetch=1,
            grid=(feats // tile,),
            in_specs=[
                *[pl.BlockSpec((CHUNK, cols), lambda i, c: (0, 0)) for r in rows],
                pl.BlockSpec((4 * CHUNK, factors.shape[1]), lambda i, c: (0, 0)),
                pl.BlockSpec((cols, tile), lambda i, c: (0, i)),
            ],
            out_specs=(out_spec, out_spec),
            scratch_shapes=[pltpu.VMEM((4 * CHUNK, cols), bf16), pltpu.VMEM((512, tile), f32)],
        ),
        compiler_params=LARGE,
        cost_estimate=pl.CostEstimate(
            flops=8 * CHUNK * cols * feats, bytes_accessed=4 * cols * feats, transcendentals=0
        ),
    )(core.reshape(1), *rows, factors, head_t)


def share(value, axes, count, groups=None):
    copies = jnp.broadcast_to(value[None], (count, *value.shape))
    return lax.all_to_all(copies, axes, 0, 0, tiled=True, axis_index_groups=groups)


def shards(hidden, norm_gain, head, token_ids, entropy_mask, group_ids, old_logp, scores):
    tokens, share_cols = hidden.shape
    feats, vocab_cols = head.shape
    section, dp = lax.axis_index(SECTION), lax.axis_index(DP)
    core, low = section % 2, section // 2
    slice_index = lax.axis_index((SECTION, VOCAB))
    head_t = head.T
    hidden_t = hidden.T.astype(f32)
    gain = norm_gain.astype(f32)[:, None]

    rest = jnp.sum(hidden_t * hidden_t, axis=0, keepdims=True)
    pieces = []
    for _ in range(3):
        pieces.append(lax.reduce_precision(rest, 8, 7))
        rest = rest - pieces[-1]
    own = jnp.concatenate([hidden_t * gain, *pieces, jnp.zeros((5, tokens), f32)]).astype(bf16)
    own = lax.ppermute(own, (SECTION, DP), SPREAD)
    lines = share(own, (SECTION, VOCAB), 8, Z_GROUPS)

    blocks = share(lines, VOCAB, 4, X_GROUPS).reshape(4, 2, 4, share_cols + 8, tokens)
    sums = jnp.sum(blocks[:, :, :, share_cols:].astype(f32), axis=(0, 2, 3))
    blocks = blocks[:, :, :, :share_cols].transpose(1, 2, 0, 3, 4).reshape(2, feats, tokens)

    def send(part):
        return lax.ppermute(part, (SECTION, DP), STEP)

    first, later = blocks[0], blocks[1]
    p1 = send(first_message(head_t, first, sums[:1], 0))
    q1 = send(first_message(head_t, first, sums[:1], 1))
    later_pair = lax.ppermute(later, SECTION, CORE_SWAP)
    first_pair = lax.ppermute(first, SECTION, CORE_SWAP)
    sums, later_pair = lax.optimization_barrier((sums, later_pair))
    sums_pair = lax.ppermute(sums, SECTION, CORE_SWAP)
    is_even = core == 0
    second_sum, last_sum = jnp.where(is_even, sums, sums_pair)[1:], jnp.where(is_even, sums_pair, sums)[1:]
    second, last = jnp.where(is_even, later, later_pair), jnp.where(is_even, later_pair, later)
    part2, part3 = lax.optimization_barrier((base(head_t, second), base(head_t, first_pair)))
    p2 = send(message(part2, second_sum, 0, p1))
    q2 = send(message(part2, second_sum, 1, q1))
    p3 = send(message(part3, sums_pair[:1], 0, p2))
    q3 = message(part3, sums_pair[:1], 1, q2)
    q3 = send(q3)
    local_target = token_ids - slice_index * vocab_cols
    local_target = jnp.where(local_target < vocab_cols, local_target, -1)

    chosen = entropy_mask != 0
    position = jnp.where(chosen, jnp.cumsum(chosen.astype(i32)) - 1, -1)
    count = jnp.sum(chosen.astype(i32))
    slots = jnp.arange(CHUNK, dtype=i32)
    pick0 = position[None, :] == slots[:, None]

    own_part = base(head_t, last)
    exps, mine0, stats = finish(
        vocab_cols, share_cols * 64, own_part, p3, q3, last_sum, local_target[None], pick0.astype(bf16)
    )

    def send_rows(mine):
        from_below = lax.ppermute(mine, DP, UP)
        from_above = lax.ppermute(mine, DP, DOWN)
        return from_above, from_below, mine

    def gather_rows(chunk):
        pick = position[None, :] == (slots + chunk * CHUNK)[:, None]
        mine = lax.dot_general(
            pick.astype(bf16), exps, (((1,), (1,)), ((), ())), preferred_element_type=f32
        ).astype(bf16)
        return pick, send_rows(mine)

    rows0 = send_rows(mine0)

    inverse = stats[4]
    every = share(stats[:4], (SECTION, VOCAB), 64)
    row_top = jnp.max(every[:, 0], axis=0)
    scale = jnp.exp(every[:, 0] - row_top)
    exp_total = jnp.sum(scale * every[:, 1], axis=0)
    weighted = jnp.sum(scale * every[:, 2], axis=0)
    target = jnp.sum(every[:, 3], axis=0)
    log_total = row_top + jnp.log(exp_total)
    mean_logit = weighted / exp_total
    entropy = log_total - mean_logit
    new_logp = target - log_total
    first_group = dp * GPD
    members = (
        group_ids[:, None] == first_group + jnp.arange(GPD, dtype=i32)[None, :]
    ).astype(f32)
    group_sum = jnp.sum(scores[:, None] * members, axis=0)
    group_count = jnp.sum(members, axis=0)
    advantage = scores - jnp.sum(members * (group_sum / group_count)[None], axis=1)
    weight = jnp.clip(jnp.exp(new_logp - old_logp), LOW_CLIP, HIGH_CLIP)
    grad_logp = -entropy_mask.astype(f32) * weight * advantage
    soft = -grad_logp * jnp.exp(stats[0] - row_top) / exp_total

    def chunk_grad(pick, rows):
        values = jnp.stack([soft, grad_logp, token_ids.astype(f32), jnp.broadcast_to(count.astype(f32), soft.shape)])
        picked = jnp.sum(jnp.where(pick[None], values[:, None, :], 0.0), axis=2)
        picked = picked.at[3].set(count.astype(f32))
        from_above, from_below, mine = rows
        across = lax.ppermute(jnp.where(core == 0, from_below, from_above), (SECTION, DP), STEP)
        rows = from_below, from_above, across, mine
        factors = share(picked, DP, 4)
        most = jnp.max(factors[:, 3, 0]).astype(i32)
        factors = jnp.stack([lax.dynamic_index_in_dim(factors, (dp + r) % 4, 0, False) for r in REL])
        factors = factors.transpose(0, 2, 1).reshape(4 * CHUNK, 4)
        factors = factors - jnp.array([0, 0, 1, 0], f32) * (slice_index * vocab_cols).astype(f32)

        keep, give = grad_product(head_t, rows, factors, core)
        part = (keep.astype(f32) + lax.ppermute(give, SECTION, CORE_SWAP).astype(f32)).astype(bf16)
        part = part.reshape(32, -1, part.shape[-1])
        part = lax.all_to_all(
            part, (SECTION, VOCAB), 0, 0, tiled=True, axis_index_groups=CORE_GROUPS
        )
        part = jnp.sum(part.astype(f32), axis=0)
        part = jnp.concatenate([part[:, :CHUNK], part[:, CHUNK:]], axis=0)
        part = lax.ppermute(part, (SECTION, DP), COLLECT)
        return jnp.dot(part, pick.astype(f32), precision=lax.Precision.HIGHEST), most

    grad, most = chunk_grad(pick0, rows0)

    def more(state):
        chunk, total = state
        part, _ = chunk_grad(*gather_rows(chunk))
        return chunk + 1, total + part

    _, grad = lax.while_loop(lambda state: state[0] * CHUNK < most, more, (jnp.ones((), i32), grad))

    inner = grad_logp * (target - mean_logit) / (share_cols * 64)
    unit = hidden_t * inverse
    grad_hidden = inverse * (gain * grad - unit * inner[None])
    return new_logp, entropy, grad_hidden.astype(bf16).T


def solution(mesh):
    in_specs = (
        P("dp", ("section", "vocab")),
        P(("section", "vocab")),
        P("dp", ("section", "vocab")),
        P("dp"),
        P("dp"),
        P("dp"),
        P("dp"),
        P("dp"),
    )
    out_specs = (P("dp"), P("dp"), P("dp", ("section", "vocab")))
    return jax.shard_map(shards, mesh=mesh, in_specs=in_specs, out_specs=out_specs, check_vma=False)
```

```python
import functools

import jax
import jax.numpy as jnp
from jax import lax
from jax.experimental import pallas as pl
from jax.experimental.pallas import tpu as pltpu
from jax.sharding import PartitionSpec as P

NORM_EPSILON = 1e-06
LOW_CLIP = 0.5
HIGH_CLIP = 2.0
GPD = 8
CHUNK = 64
SHARE = 80
TILE = 1200
EXTRA = 16
HALF_TILES = 1
BIG = 32000.0
REL = (3, 1, 2, 0)
SECTION, DP, VOCAB = "section", "dp", "vocab"
f32, bf16, i16, i32 = jnp.float32, jnp.bfloat16, jnp.int16, jnp.int32
CORE_SWAP = ((0, 1), (1, 0), (2, 3), (3, 2))
UP = tuple((i, (i + 1) % 4) for i in range(4))
DOWN = tuple((i, (i + 3) % 4) for i in range(4))
X_GROUPS = [[z * 4 + x for x in range(4)] for z in range(4)]
Z_GROUPS = [[(a * 2 + c) * 16 + b * 4 + x for a in range(2) for b in range(4)] for c in range(2) for x in range(4)]
STEP = tuple((s * 4 + d, s * 4 + (d + (3 if s % 2 else 1)) % 4) for s in range(4) for d in range(4))
CORE_GROUPS = [[(z * 2 + c) * 16 + v for z in range(2) for v in range(16)] for c in range(2)]
SPREAD = tuple((d * 4 + (d + REL[s]) % 4, s * 4 + d) for s in range(4) for d in range(4))
COLLECT = tuple((b, a) for a, b in SPREAD)
SMALL = pltpu.CompilerParams(vmem_limit_bytes=10 * 1024 * 1024)
LARGE = pltpu.CompilerParams(vmem_limit_bytes=15 * 1024 * 1024)


def decode(block):
    codes = block[:TILE].astype(f32)
    power = block[TILE : TILE + EXTRA].astype(f32)[:1]
    return codes * (jnp.exp2(power - 15.0) * (32768.0 / BIG))


def encode(part, square_sum, out_ref, tile):
    start = tile * (TILE + EXTRA)
    top = jnp.max(jnp.abs(part), axis=0, keepdims=True)
    power = jnp.clip(jnp.floor(jnp.log2(jnp.maximum(top, 1e-30))) + 1.0, -90.0, 90.0)
    codes = part * (jnp.exp2(15.0 - power) * (BIG / 32768.0))
    codes = jnp.clip(jnp.round(codes), -32767.0, 32767.0)
    sum_power = jnp.clip(jnp.floor(jnp.log2(jnp.maximum(square_sum, 1e-30))) + 1.0, -100.0, 100.0)
    scaled = square_sum * jnp.exp2(15.0 - sum_power)
    high = jnp.minimum(jnp.floor(scaled), 32767.0)
    spare = jnp.zeros((EXTRA - 4, part.shape[1]), f32)
    extra = jnp.concatenate([power, sum_power, high, jnp.round((scaled - high) * 16384.0), spare], axis=0)
    out_ref[start : start + TILE] = codes.astype(i32).astype(i16)
    out_ref[start + TILE : start + TILE + EXTRA] = extra.astype(i32).astype(i16)


def decode_sum(block):
    extra = block[TILE : TILE + EXTRA].astype(f32)
    return (extra[2:3] + extra[3:4] * (1.0 / 16384.0)) * jnp.exp2(extra[1:2] - 15.0)


def inside(part, rows, start):
    index = lax.broadcasted_iota(i32, part.shape, 0) + start
    return jnp.where(index < rows, part, 0.0)


def first_kernel(rows, half, head_ref, x_ref, sum_ref, out_ref):
    for tile in range(HALF_TILES):
        at = tile * TILE
        part = jnp.dot(head_ref[at : at + TILE], x_ref[...], preferred_element_type=f32)
        if (half * HALF_TILES + tile + 1) * TILE > rows:
            part = inside(part, rows, (half * HALF_TILES + tile) * TILE)
        encode(part, sum_ref[...], out_ref, tile)


def first_message(head_t, x, square_sum, half):
    rows, feats = head_t.shape
    tokens = x.shape[1]
    block = TILE + EXTRA
    whole = lambda i: (0, 0)
    return pl.pallas_call(
        functools.partial(first_kernel, rows, half),
        out_shape=jax.ShapeDtypeStruct((HALF_TILES * block, tokens), i16),
        grid=(1,),
        in_specs=[
            pl.BlockSpec((HALF_TILES * TILE, feats), lambda i: (half, 0)),
            pl.BlockSpec((feats, tokens), whole),
            pl.BlockSpec((1, tokens), whole),
        ],
        out_specs=pl.BlockSpec((HALF_TILES * block, tokens), whole),
        compiler_params=SMALL,
        cost_estimate=pl.CostEstimate(
            flops=rows * feats * tokens, bytes_accessed=4 * rows * feats, transcendentals=0
        ),
    )(head_t, x, square_sum)


def message_kernel(half, part_ref, sum_ref, arrived_ref, out_ref):
    block = TILE + EXTRA
    for tile in range(HALF_TILES):
        at = (half * HALF_TILES + tile) * TILE
        arrived = arrived_ref[tile * block : (tile + 1) * block]
        encode(part_ref[at : at + TILE] + decode(arrived), sum_ref[...] + decode_sum(arrived), out_ref, tile)


def message(part, square_sum, half, arrived):
    return pl.pallas_call(
        functools.partial(message_kernel, half),
        out_shape=jax.ShapeDtypeStruct(arrived.shape, i16),
        compiler_params=SMALL,
        cost_estimate=pl.CostEstimate(
            flops=8 * arrived.size, bytes_accessed=8 * arrived.size, transcendentals=0
        ),
    )(part, square_sum, arrived)


def base_kernel(rows, head_ref, x_ref, out_ref):
    part = jnp.dot(head_ref[...], x_ref[...], preferred_element_type=f32)
    out_ref[...] = inside(part, rows, pl.program_id(0) * HALF_TILES * TILE)


def base(head_t, x):
    rows, feats = head_t.shape
    tokens = x.shape[1]
    return pl.pallas_call(
        functools.partial(base_kernel, rows),
        out_shape=jax.ShapeDtypeStruct((2 * HALF_TILES * TILE, tokens), f32),
        grid=(2,),
        in_specs=[
            pl.BlockSpec((HALF_TILES * TILE, feats), lambda i: (i, 0)),
            pl.BlockSpec((feats, tokens), lambda i: (0, 0)),
        ],
        out_specs=pl.BlockSpec((HALF_TILES * TILE, tokens), lambda i: (i, 0)),
        compiler_params=LARGE,
        cost_estimate=pl.CostEstimate(
            flops=2 * rows * feats * tokens, bytes_accessed=2 * rows * feats, transcendentals=0
        ),
    )(head_t, x)


def finish_kernel(rows, feats, base_ref, a_ref, b_ref, sum_ref, target_ref, pick_ref, e_ref, mine_ref, stats_ref, logits, exps):
    tokens = base_ref.shape[1]
    block = TILE + EXTRA
    square_sum = sum_ref[...] + decode_sum(a_ref[:block, :])
    inverse = lax.rsqrt(square_sum / feats + NORM_EPSILON)
    top = jnp.full((1, tokens), -1e30, f32)
    for tile in range(2 * HALF_TILES):
        at = tile * TILE
        ref, place = (a_ref, tile) if tile < HALF_TILES else (b_ref, tile - HALF_TILES)
        value = (base_ref[at : at + TILE, :] + decode(ref[place * block : (place + 1) * block, :])) * inverse
        if at + TILE > rows:
            index = lax.broadcasted_iota(i32, value.shape, 0) + at
            value = jnp.where(index < rows, value, -1e30)
        logits[at : at + TILE, :] = value
        top = jnp.maximum(top, jnp.max(value, axis=0, keepdims=True))
    total = jnp.zeros((1, tokens), f32)
    weighted = jnp.zeros((1, tokens), f32)
    target = jnp.zeros((1, tokens), f32)
    place = lax.broadcasted_iota(i32, (TILE, tokens), 0)
    for tile in range(2 * HALF_TILES):
        at = tile * TILE
        value = logits[at : at + TILE, :]
        e = jnp.exp(value - top)
        total += jnp.sum(e, axis=0, keepdims=True)
        weighted += jnp.sum(e * value, axis=0, keepdims=True)
        target += jnp.sum(jnp.where(place == target_ref[...] - at, value, 0.0), axis=0, keepdims=True)
        exps[at : at + TILE, :] = e.astype(bf16)
    spare = exps.shape[0] - 2 * HALF_TILES * TILE
    exps[2 * HALF_TILES * TILE :, :] = jnp.zeros((spare, tokens), bf16)
    stats_ref[...] = jnp.concatenate([top, total, weighted, target, inverse], axis=0)
    mine = lax.dot_general(pick_ref[...], exps[...], (((1,), (1,)), ((), ())), preferred_element_type=f32)
    mine_ref[...] = mine[:, :rows].astype(bf16)
    e_ref[...] = exps[:rows, :]


def finish(rows, feats, total, a, b, square_sum, target, pick):
    tokens = total.shape[1]
    padded = -(-rows // 128) * 128
    return pl.pallas_call(
        functools.partial(finish_kernel, rows, float(feats)),
        out_shape=(
            jax.ShapeDtypeStruct((rows, tokens), bf16),
            jax.ShapeDtypeStruct((CHUNK, rows), bf16),
            jax.ShapeDtypeStruct((5, tokens), f32),
        ),
        scratch_shapes=[pltpu.VMEM((2 * HALF_TILES * TILE, tokens), f32), pltpu.VMEM((padded, tokens), bf16)],
        compiler_params=LARGE,
        cost_estimate=pl.CostEstimate(
            flops=2 * rows * CHUNK * tokens, bytes_accessed=10 * rows * tokens, transcendentals=rows * tokens
        ),
    )(total, a, b, square_sum, target, pick)


def grad_kernel(rows, core_ref, r0, r1, r2, r3, factor_ref, head_ref, keep_ref, give_ref, left, prod):
    @pl.when(pl.program_id(0) == 0)
    def _():
        for t, ref in enumerate((r0, r1, r2, r3)):
            factor = factor_ref[t * CHUNK : (t + 1) * CHUNK, :]
            index = lax.broadcasted_iota(i32, (CHUNK, rows), 1)
            hard = jnp.where(index == factor[:, 2:3].astype(i32), factor[:, 1:2], 0.0)
            value = ref[...].astype(f32) * factor[:, 0:1] + hard
            left[t * CHUNK : (t + 1) * CHUNK, :] = value.astype(bf16)

    out = jnp.dot(left[...], head_ref[...], preferred_element_type=f32)
    for t in range(4):
        prod[t * 128 : t * 128 + CHUNK, :] = out[t * CHUNK : (t + 1) * CHUNK]
    core = core_ref[0]
    tile = head_ref.shape[1]
    for z in range(2):
        for ref, side in ((keep_ref, core), (give_ref, 1 - core)):
            at = pl.multiple_of((z * 2 + side) * 128, 128)
            turned = prod[pl.ds(at, 128), :].T
            lane = lax.broadcasted_iota(i32, (SHARE // 2, 128), 1)
            for group in range(tile // SHARE):
                top = turned[group * SHARE : group * SHARE + SHARE // 2]
                low = turned[group * SHARE + SHARE // 2 : (group + 1) * SHARE]
                packed = jnp.where(lane < CHUNK, top, pltpu.roll(low, CHUNK, 1))
                ref[z, group * SHARE // 2 : (group + 1) * SHARE // 2] = packed.astype(bf16)


def grad_product(head_t, rows, factors, core):
    cols, feats = head_t.shape
    tile = feats
    out = jax.ShapeDtypeStruct((2, feats // 2, 128), bf16)
    out_spec = pl.BlockSpec((2, tile // 2, 128), lambda i, c: (0, i, 0))
    return pl.pallas_call(
        functools.partial(grad_kernel, cols),
        out_shape=(out, out),
        grid_spec=pltpu.PrefetchScalarGridSpec(
            num_scalar_prefetch=1,
            grid=(feats // tile,),
            in_specs=[
                *[pl.BlockSpec((CHUNK, cols), lambda i, c: (0, 0)) for r in rows],
                pl.BlockSpec((4 * CHUNK, factors.shape[1]), lambda i, c: (0, 0)),
                pl.BlockSpec((cols, tile), lambda i, c: (0, i), pipeline_mode=pl.Buffered(1)),
            ],
            out_specs=(out_spec, out_spec),
            scratch_shapes=[pltpu.VMEM((4 * CHUNK, cols), bf16), pltpu.VMEM((512, tile), f32)],
        ),
        compiler_params=LARGE,
        cost_estimate=pl.CostEstimate(
            flops=8 * CHUNK * cols * feats, bytes_accessed=4 * cols * feats, transcendentals=0
        ),
    )(core.reshape(1), *rows, factors, head_t)


def share(value, axes, count, groups=None):
    copies = jnp.broadcast_to(value[None], (count, *value.shape))
    return lax.all_to_all(copies, axes, 0, 0, tiled=True, axis_index_groups=groups)


def shards(hidden, norm_gain, head, token_ids, entropy_mask, group_ids, old_logp, scores):
    tokens, share_cols = hidden.shape
    feats, vocab_cols = head.shape
    section, dp = lax.axis_index(SECTION), lax.axis_index(DP)
    core, low = section % 2, section // 2
    slice_index = lax.axis_index((SECTION, VOCAB))
    head_t = head.T
    hidden_t = hidden.T.astype(f32)
    gain = norm_gain.astype(f32)[:, None]

    rest = jnp.sum(hidden_t * hidden_t, axis=0, keepdims=True)
    pieces = []
    for _ in range(3):
        pieces.append(lax.reduce_precision(rest, 8, 7))
        rest = rest - pieces[-1]
    own = jnp.concatenate([hidden_t * gain, *pieces, jnp.zeros((5, tokens), f32)]).astype(bf16)
    own = lax.ppermute(own, (SECTION, DP), SPREAD)
    lines = share(own, (SECTION, VOCAB), 8, Z_GROUPS)

    blocks = share(lines, VOCAB, 4, X_GROUPS).reshape(4, 2, 4, share_cols + 8, tokens)
    sums = jnp.sum(blocks[:, :, :, share_cols:].astype(f32), axis=(0, 2, 3))
    blocks = blocks[:, :, :, :share_cols].transpose(1, 2, 0, 3, 4).reshape(2, feats, tokens)

    def send(part):
        return lax.ppermute(part, (SECTION, DP), STEP)

    first, later = blocks[0], blocks[1]
    p1 = send(first_message(head_t, first, sums[:1], 0))
    q1 = send(first_message(head_t, first, sums[:1], 1))
    later_pair = lax.ppermute(later, SECTION, CORE_SWAP)
    first_pair = lax.ppermute(first, SECTION, CORE_SWAP)
    sums, later_pair = lax.optimization_barrier((sums, later_pair))
    sums_pair = lax.ppermute(sums, SECTION, CORE_SWAP)
    is_even = core == 0
    second_sum, last_sum = jnp.where(is_even, sums, sums_pair)[1:], jnp.where(is_even, sums_pair, sums)[1:]
    second, last = jnp.where(is_even, later, later_pair), jnp.where(is_even, later_pair, later)
    part2, part3 = lax.optimization_barrier((base(head_t, second), base(head_t, first_pair)))
    p2 = send(message(part2, second_sum, 0, p1))
    q2 = send(message(part2, second_sum, 1, q1))
    p3 = send(message(part3, sums_pair[:1], 0, p2))
    q3 = message(part3, sums_pair[:1], 1, q2)
    q3 = send(q3)
    local_target = token_ids - slice_index * vocab_cols
    local_target = jnp.where(local_target < vocab_cols, local_target, -1)

    chosen = entropy_mask != 0
    position = jnp.where(chosen, jnp.cumsum(chosen.astype(i32)) - 1, -1)
    count = jnp.sum(chosen.astype(i32))
    slots = jnp.arange(CHUNK, dtype=i32)
    pick0 = position[None, :] == slots[:, None]

    own_part = base(head_t, last)
    exps, mine0, stats = finish(
        vocab_cols, share_cols * 64, own_part, p3, q3, last_sum, local_target[None], pick0.astype(bf16)
    )

    def send_rows(mine):
        from_below = lax.ppermute(mine, DP, UP)
        from_above = lax.ppermute(mine, DP, DOWN)
        return from_above, from_below, mine

    def gather_rows(chunk):
        pick = position[None, :] == (slots + chunk * CHUNK)[:, None]
        mine = lax.dot_general(
            pick.astype(bf16), exps, (((1,), (1,)), ((), ())), preferred_element_type=f32
        ).astype(bf16)
        return pick, send_rows(mine)

    rows0 = send_rows(mine0)

    inverse = stats[4]
    every = share(stats[:4], (SECTION, VOCAB), 64)
    row_top = jnp.max(every[:, 0], axis=0)
    scale = jnp.exp(every[:, 0] - row_top)
    exp_total = jnp.sum(scale * every[:, 1], axis=0)
    weighted = jnp.sum(scale * every[:, 2], axis=0)
    target = jnp.sum(every[:, 3], axis=0)
    log_total = row_top + jnp.log(exp_total)
    mean_logit = weighted / exp_total
    entropy = log_total - mean_logit
    new_logp = target - log_total
    first_group = dp * GPD
    members = (
        group_ids[:, None] == first_group + jnp.arange(GPD, dtype=i32)[None, :]
    ).astype(f32)
    group_sum = jnp.sum(scores[:, None] * members, axis=0)
    group_count = jnp.sum(members, axis=0)
    advantage = scores - jnp.sum(members * (group_sum / group_count)[None], axis=1)
    weight = jnp.clip(jnp.exp(new_logp - old_logp), LOW_CLIP, HIGH_CLIP)
    grad_logp = -entropy_mask.astype(f32) * weight * advantage
    soft = -grad_logp * jnp.exp(stats[0] - row_top) / exp_total

    def chunk_grad(pick, rows):
        values = jnp.stack([soft, grad_logp, token_ids.astype(f32), jnp.broadcast_to(count.astype(f32), soft.shape)])
        picked = jnp.sum(jnp.where(pick[None], values[:, None, :], 0.0), axis=2)
        picked = picked.at[3].set(count.astype(f32))
        from_above, from_below, mine = rows
        across = lax.ppermute(jnp.where(core == 0, from_below, from_above), (SECTION, DP), STEP)
        rows = from_below, from_above, across, mine
        factors = share(picked, DP, 4)
        most = jnp.max(factors[:, 3, 0]).astype(i32)
        factors = jnp.stack([lax.dynamic_index_in_dim(factors, (dp + r) % 4, 0, False) for r in REL])
        factors = factors.transpose(0, 2, 1).reshape(4 * CHUNK, 4)
        factors = factors - jnp.array([0, 0, 1, 0], f32) * (slice_index * vocab_cols).astype(f32)

        keep, give = grad_product(head_t, rows, factors, core)
        part = (keep.astype(f32) + lax.ppermute(give, SECTION, CORE_SWAP).astype(f32)).astype(bf16)
        part = part.reshape(32, -1, part.shape[-1])
        part = lax.all_to_all(
            part, (SECTION, VOCAB), 0, 0, tiled=True, axis_index_groups=CORE_GROUPS
        )
        part = jnp.sum(part.astype(f32), axis=0)
        part = jnp.concatenate([part[:, :CHUNK], part[:, CHUNK:]], axis=0)
        part = lax.ppermute(part, (SECTION, DP), COLLECT)
        return jnp.dot(part, pick.astype(f32), precision=lax.Precision.HIGHEST), most

    grad, most = chunk_grad(pick0, rows0)

    def more(state):
        chunk, total = state
        part, _ = chunk_grad(*gather_rows(chunk))
        return chunk + 1, total + part

    _, grad = lax.while_loop(lambda state: state[0] * CHUNK < most, more, (jnp.ones((), i32), grad))

    inner = grad_logp * (target - mean_logit) / (share_cols * 64)
    unit = hidden_t * inverse
    grad_hidden = inverse * (gain * grad - unit * inner[None])
    return new_logp, entropy, grad_hidden.astype(bf16).T


def solution(mesh):
    in_specs = (
        P("dp", ("section", "vocab")),
        P(("section", "vocab")),
        P("dp", ("section", "vocab")),
        P("dp"),
        P("dp"),
        P("dp"),
        P("dp"),
        P("dp"),
    )
    out_specs = (P("dp"), P("dp"), P("dp", ("section", "vocab")))
    return jax.shard_map(shards, mesh=mesh, in_specs=in_specs, out_specs=out_specs, check_vma=False)
```
